32 devices in a mesh: grp: 2 (over x), band: 16 (over z, y, core).
Axes of the slice: x: 2, y: 2, z: 4, core: 2. Of those that a mesh axis runs over, the one named last changes fastest.
Arguments:
- node_lat: bfloat16 [8192, 256], P(('grp', 'band')), parts along dimension 0, may hold values from -6 to 6
- edge_lat: bfloat16 [163840, 256], P(('grp', 'band')), parts along dimension 0, may hold values from -6 to 6
- node_cot: bfloat16 [8192, 256], P(('grp', 'band')), parts along dimension 0, may hold values from -6 to 6
- edge_cot: bfloat16 [163840, 256], P(('grp', 'band')), parts along dimension 0, may hold values from -6 to 6
- w_edge_in: bfloat16 [768, 256], replicated, may hold values from -0.21875 to 0.21875
- w_edge_out: bfloat16 [256, 256], replicated, may hold values from -0.375 to 0.375
- gain_edge: float32 [256], replicated, may hold values from 0.25 to 1.75
- w_node_in: bfloat16 [512, 256], replicated, may hold values from -0.25 to 0.25
- w_node_out: bfloat16 [256, 256], replicated, may hold values from -0.375 to 0.375
- gain_node: float32 [256], replicated, may hold values from 0.25 to 1.75
- fetch_idx: int32 [16, 16, 32], P('band'), may hold values from 0 to 255
- edge_slot: int32 [81920], P('band'), may hold values from 0 to 511
- edge_recv: int32 [81920], P('band'), may hold values from 0 to 255
- block_fill: int32 [16, 40], P('band'), may hold values from 1 to 128, 3840 in all within a row
Outputs:
- node_grad: float32 [8192, 256], P(('grp', 'band')), parts along dimension 0
- edge_grad: bfloat16 [163840, 256], P(('grp', 'band')), parts along dimension 0
- w_edge_in_grad: float32 [1536, 256], P('grp'), parts along dimension 0
- w_edge_out_grad: float32 [512, 256], P('grp'), parts along dimension 0
- gain_edge_grad: float32 [512], P('grp'), parts along dimension 0
- w_node_in_grad: float32 [1024, 256], P('grp'), parts along dimension 0
- w_node_out_grad: float32 [512, 256], P('grp'), parts along dimension 0
- gain_node_grad: float32 [512], P('grp'), parts along dimension 0
The draws below stay inside these ranges and needn't reach their ends.
There are 2 independent parts, one for each index of `grp`. The reference program is written for one: setup_inputs(seed, part) draws one part's arguments, and reference() takes and returns one part's arrays. A program takes and returns all parts, laid end to end along the dimension named above; an argument that names none is the same for every part. Nothing has to cross between parts.
Inputs may be any that keep to these rules, and one draw needn't show every extreme that they name: `fetch_idx`: entries of one list may repeat; every entry of every list is a real node. `block_fill`: the blocks of one patch hold 3840 live edges together, and some block is full.
All inputs are finite; a program needn't handle non-finite values.
Results may differ from the reference program's by a relative error of at most 0.0075.
Values may be sent and summed in bfloat16 or wider, within the bound.
No kernel may reach another device: no remote copies, remote signals or barrier semaphores. Data moves between devices by JAX's collectives and lax.ppermute only.
A program may use at most 192 MiB of HBM per device.

```python
import math
import jax
import jax.numpy as jnp
import numpy as np
from jax import lax

L = 256
H = 256
NODE_DEV = 256
BLK = 40
CAP = 32
NODES = 4096
EDGES = 81920
N_BAND = 16


def with_ends(array, stream_key, least, top_value):
    index_at = [jax.random.randint(jax.random.fold_in(stream_key, axis), (), 0, length) for axis, length in enumerate(array.shape)]
    widest = array.shape.index(max(array.shape))
    neighbour = index_at[:widest] + [(index_at[widest] + 1) % array.shape[widest]] + index_at[widest + 1:]
    return array.at[tuple(index_at)].set(least).at[tuple(neighbour)].set(top_value)


def shard_levels(rng, dims, shards, low, top_value):
    loudness, own = 1.0, jax.random.fold_in(rng, 6)
    for position, parts in shards:
        steps = jnp.exp(jax.random.uniform(jax.random.fold_in(own, position), (parts,), jnp.float32, low / len(shards), top_value / len(shards)))
        loudness = loudness * jnp.repeat(steps, dims[position] // parts).reshape([-1 if axis == position else 1 for axis in range(len(dims))])
    return loudness


def length_profile(count, total, reach, slope):
    weights = [(1 << 20) // math.isqrt(standing ** slope) + 1 for standing in range(2, count + 1)]
    spare, counts = total - reach - (count - 1), [1] * (count - 1)
    while spare > 0:
        movable = [i for i in range(count - 1) if counts[i] < reach]
        whole, left = sum([weights[i] for i in movable]), spare
        for i in movable:
            addition = min(reach - counts[i], max(1, left * weights[i] // whole), spare)
            counts[i] = counts[i] + addition
            spare = spare - addition
    return np.array([reach] + counts)


def uneven(own_key, number_of, total, most, lean):
    if number_of == 2:
        one = jax.random.randint(own_key, (), max(1, total - most), min(most, total - 1) + 1)
        return jnp.stack([one, total - one])
    tallies = jnp.asarray(length_profile(number_of, total, most, lean), jnp.int32)
    twos = (number_of - 1) // 2
    donor, taker = tallies[1:1 + 2 * twos:2], tallies[2:2 + 2 * twos:2]
    slack = jnp.minimum(donor - 1, most - taker)
    moved = jax.random.randint(jax.random.fold_in(own_key, 1), (twos,), 0, 1 << 20) % (slack + 1)
    tallies = tallies.at[1:1 + 2 * twos:2].set(donor - moved).at[2:2 + 2 * twos:2].set(taker + moved)
    return tallies[jax.random.permutation(jax.random.fold_in(own_key, 2), number_of)]


def gaussian(own_key, shape, spread, bound, cuts=(), kind=jnp.bfloat16):
    loudness = shard_levels(own_key, shape, cuts, -0.22, 0.18) if cuts else 1.0
    entries = jax.random.normal(own_key, shape, jnp.float32) * spread * loudness
    return jnp.minimum(jnp.maximum(entries, -bound), bound).astype(kind)


def setup_inputs(seed: int = 0, part: int = 0) -> dict:
    seeds = jax.random.split(jax.random.key(seed), 15)
    part_splits = jax.random.split(jax.random.fold_in(seeds[14], part), 15)
    return {
        "node_lat": gaussian(part_splits[0], (NODES, L), 1.0, 6.0, ((0, 16),)),
        "edge_lat": gaussian(part_splits[1], (EDGES, L), 1.0, 6.0, ((0, 16),)),
        "node_cot": gaussian(part_splits[2], (NODES, L), 1.0, 6.0, ((0, 16),)),
        "edge_cot": gaussian(part_splits[3], (EDGES, L), 1.0, 6.0, ((0, 16),)),
        "w_edge_in": gaussian(seeds[4], (3 * L, H), (3 * L) ** -0.5, 0.21875),
        "w_edge_out": gaussian(seeds[5], (H, L), H ** -0.5, 0.375),
        "gain_edge": jnp.clip(1.0 + 0.15 * jax.random.normal(seeds[6], (L,), jnp.float32), 0.25, 1.75),
        "w_node_in": gaussian(seeds[7], (2 * L, H), (2 * L) ** -0.5, 0.25),
        "w_node_out": gaussian(seeds[8], (H, L), H ** -0.5, 0.375),
        "gain_node": jnp.clip(1.0 + 0.15 * jax.random.normal(seeds[9], (L,), jnp.float32), 0.25, 1.75),
        "fetch_idx": with_ends(jax.random.randint(seeds[10], (N_BAND, N_BAND, CAP), 0, NODE_DEV), jax.random.fold_in(seeds[10], 1), 0, NODE_DEV - 1).astype(jnp.int32),
        "edge_slot": with_ends(jax.random.randint(seeds[11], (EDGES,), 0, N_BAND * CAP), jax.random.fold_in(seeds[11], 1), 0, (N_BAND * CAP) - 1).astype(jnp.int32),
        "edge_recv": with_ends(jax.random.randint(seeds[12], (EDGES,), 0, NODE_DEV), jax.random.fold_in(seeds[12], 1), 0, NODE_DEV - 1).astype(jnp.int32),
        "block_fill": jax.vmap(lambda own: uneven(own, BLK, BLK * 96, 128, 1))(jax.random.split(seeds[13], N_BAND)).reshape((N_BAND, BLK)).astype(jnp.int32),
    }


epsilon = 1e-05

def swish(values):
    return values * jax.nn.sigmoid(values)

def swish_slope(values):
    logistic = jax.nn.sigmoid(values)
    return logistic * (1.0 + values * (1.0 - logistic))

def normalize(values):
    centred = values - lax.optimization_barrier(jnp.mean(values, axis=-1, keepdims=True))
    scale_inv = lax.rsqrt(lax.optimization_barrier(jnp.mean(centred * centred, axis=-1, keepdims=True)) + epsilon)
    return (centred * scale_inv, scale_inv)

def normalize_back(incoming, normed, scale_inv, gain_vec):
    scaled = incoming * gain_vec
    return scale_inv * (scaled - lax.optimization_barrier(jnp.mean(scaled, axis=-1, keepdims=True)) - normed * lax.optimization_barrier(jnp.mean(scaled * normed, axis=-1, keepdims=True)))

def matmul(lhs_mat, rhs_mat):
    return jnp.dot(lhs_mat, rhs_mat, preferred_element_type=jnp.float32)

def patch_backward(node_own, senders, edge_own, recv_rows, valid, node_cotan, edge_cotan, w_edge_in, w_edge_out, gain_edge, w_node_in, w_node_out, gain_node):
    latent = node_own.shape[1]
    node_count = node_own.shape[0]
    receivers = node_own[recv_rows]
    stacked = jnp.concatenate([edge_own, senders, receivers], axis=1)
    pre_edge = matmul(stacked, w_edge_in)
    hidden_edge = swish(pre_edge).astype(jnp.bfloat16)
    out_edge = matmul(hidden_edge, w_edge_out)
    normed_edge, inv_edge = normalize(out_edge)
    valid_col = valid[:, None]
    update = normed_edge * gain_edge * valid_col
    summed = jax.ops.segment_sum(update, recv_rows, num_segments=node_count).astype(jnp.bfloat16)
    node_input = jnp.concatenate([node_own, summed], axis=1)
    pre_node = matmul(node_input, w_node_in)
    hidden_node = swish(pre_node).astype(jnp.bfloat16)
    out_node = matmul(hidden_node, w_node_out)
    normed_node, inv_node = normalize(out_node)
    node_base = node_cotan.astype(jnp.float32)
    gain_node_grad = lax.optimization_barrier(jnp.sum(node_base * normed_node, axis=0))
    grad_out_node = normalize_back(node_base, normed_node, inv_node, gain_node).astype(jnp.bfloat16)
    w_node_out_grad = matmul(hidden_node.T, grad_out_node)
    grad_pre_node = (matmul(grad_out_node, w_node_out.T) * swish_slope(pre_node)).astype(jnp.bfloat16)
    w_node_in_grad = matmul(node_input.T, grad_pre_node)
    grad_node_input = matmul(grad_pre_node, w_node_in.T)
    grad_summed = grad_node_input[:, latent:]
    edge_base = edge_cotan.astype(jnp.float32)
    grad_update = edge_base + grad_summed[recv_rows]
    gain_edge_grad = lax.optimization_barrier(jnp.sum(grad_update * normed_edge * valid_col, axis=0))
    grad_out_edge = (normalize_back(grad_update, normed_edge, inv_edge, gain_edge) * valid_col).astype(jnp.bfloat16)
    w_edge_out_grad = matmul(hidden_edge.T, grad_out_edge)
    grad_pre_edge = (matmul(grad_out_edge, w_edge_out.T) * swish_slope(pre_edge)).astype(jnp.bfloat16)
    w_edge_in_grad = matmul(stacked.T, grad_pre_edge)
    grad_stacked = matmul(grad_pre_edge, w_edge_in.T)
    edge_result = (edge_base + grad_stacked[:, :latent]).astype(jnp.bfloat16)
    node_local = node_base + grad_node_input[:, :latent] + jax.ops.segment_sum(grad_stacked[:, 2 * latent:], recv_rows, num_segments=node_count)
    weight_terms = (w_edge_in_grad, w_edge_out_grad, gain_edge_grad, w_node_in_grad, w_node_out_grad, gain_node_grad)
    return (edge_result, node_local, grad_stacked[:, latent:2 * latent], weight_terms)

def reference(node_lat, edge_lat, node_cot, edge_cot, w_edge_in, w_edge_out, gain_edge, w_node_in, w_node_out, gain_node, fetch_idx, edge_slot, edge_recv, block_fill):
    latent = node_lat.shape[1]
    edge_dev = BLK * 128
    offsets = (jnp.arange(N_BAND, dtype=jnp.int32) * NODE_DEV)[None, :, None]
    global_lists = (fetch_idx + offsets).reshape(N_BAND, N_BAND * CAP).astype(jnp.int32)
    inputs = (node_lat.reshape(N_BAND, NODE_DEV, latent), edge_lat.reshape(N_BAND, edge_dev, latent), node_cot.reshape(N_BAND, NODE_DEV, latent), edge_cot.reshape(N_BAND, edge_dev, latent), edge_slot.reshape(N_BAND, edge_dev), edge_recv.reshape(N_BAND, edge_dev), block_fill, global_lists)

    def visit(state_pair, patch_item):
        gathered_sum, weight_sums = state_pair
        node_own, edge_own, node_cotan, edge_cotan, slot_rows, recv_rows, fill_row, list_row = patch_item
        sender_ids = list_row[slot_rows]
        senders = node_lat[sender_ids]
        valid = (jnp.arange(128, dtype=jnp.int32)[None, :] < fill_row[:, None]).reshape(-1).astype(jnp.float32)
        edge_result, node_local, grad_send, weight_terms = patch_backward(node_own, senders, edge_own, recv_rows, valid, node_cotan, edge_cotan, w_edge_in, w_edge_out, gain_edge, w_node_in, w_node_out, gain_node)
        gathered_sum = gathered_sum.at[sender_ids].add(grad_send)
        weight_sums = tuple((total_now + term_now for total_now, term_now in zip(weight_sums, weight_terms)))
        return ((gathered_sum, weight_sums), (edge_result, node_local))
    hidden_units = w_edge_in.shape[1]
    start_sums = (jnp.zeros((3 * latent, hidden_units), jnp.float32), jnp.zeros((hidden_units, latent), jnp.float32), jnp.zeros((latent,), jnp.float32), jnp.zeros((2 * latent, hidden_units), jnp.float32), jnp.zeros((hidden_units, latent), jnp.float32), jnp.zeros((latent,), jnp.float32))
    start_nodes = jnp.zeros((N_BAND * NODE_DEV, latent), jnp.float32)
    (gathered_sum, weight_sums), (edge_results, node_locals) = lax.scan(visit, (start_nodes, start_sums), inputs)
    node_grad = node_locals.reshape(-1, latent) + gathered_sum
    return (node_grad, edge_results.reshape(-1, latent), weight_sums[0], weight_sums[1], weight_sums[2], weight_sums[3], weight_sums[4], weight_sums[5])
```

```python
import functools

import jax
import jax.numpy as jnp
from jax import lax
from jax.experimental import pallas as pl
from jax.experimental.pallas import tpu as pltpu
from jax.sharding import PartitionSpec as P

epsilon = 1e-05
CHUNK = 512
VMEM_LIMIT = 60 * 2**20
BF = jnp.bfloat16
F32 = jnp.float32


def dot(lhs, rhs, lhs_dim, rhs_dim):
    return lax.dot_general(
        lhs, rhs, (((lhs_dim,), (rhs_dim,)), ((), ())), preferred_element_type=F32
    )


def swish_and_slope(values):
    logistic = jax.nn.sigmoid(values)
    hidden = values * logistic
    return hidden, logistic + hidden * (1.0 - logistic)


def onehot_rows(row_count, index_row):
    rows = lax.broadcasted_iota(jnp.int32, (row_count, index_row.shape[1]), 0)
    return (rows == index_row).astype(BF)


def vmem():
    return pl.BlockSpec(memory_space=pltpu.VMEM)


def whole(shape):
    return pl.BlockSpec(shape, lambda *_: (0,) * len(shape))


def serve_kernel(asked_ref, node_ref, rows_ref):
    picks = onehot_rows(node_ref.shape[0], asked_ref[...])
    rows_ref[...] = dot(picks, node_ref[...], 0, 0).astype(BF)


def serve(asked_row, node_lat):
    return pl.pallas_call(
        serve_kernel,
        out_shape=jax.ShapeDtypeStruct((asked_row.shape[1], node_lat.shape[1]), BF),
        in_specs=[vmem(), vmem()],
        out_specs=vmem(),
        name="serve_rows",
    )(asked_row, node_lat)


def prepare_kernel(
    edge_ref, cot_ref, recv_ref, slot_ref, node_ref, w_in_t_ref, part_ref, cot_t_ref, hot_ref, node_part
):
    latent = edge_ref.shape[1]
    nodes = node_ref.shape[0]
    slots = hot_ref.shape[1] - nodes

    @pl.when(pl.program_id(0) == 0)
    def _():
        node_part[...] = dot(w_in_t_ref[:, 2 * latent :], node_ref[...], 1, 1).astype(BF)

    recv_hot = onehot_rows(nodes, recv_ref[0])
    hot_ref[0, :nodes, :] = recv_hot
    hot_ref[0, nodes:, :] = onehot_rows(slots, slot_ref[0])
    part_ref[0] = (
        dot(w_in_t_ref[:, :latent], edge_ref[...], 1, 1) + dot(node_part[...], recv_hot, 1, 0)
    ).astype(BF)
    cot_t_ref[0] = cot_ref[...].T


def prepare(edge_lat, edge_cot, recv_rows, slot_rows, node_lat, w_edge_in_t, slots):
    edges, latent = edge_lat.shape
    hidden = w_edge_in_t.shape[0]
    nodes = node_lat.shape[0]
    chunks = edges // CHUNK
    rows = pl.BlockSpec((CHUNK, latent), lambda i: (i, 0))
    index = pl.BlockSpec((1, 1, CHUNK), lambda i: (i, 0, 0))

    def out(height):
        return pl.BlockSpec((1, height, CHUNK), lambda i: (i, 0, 0))

    return pl.pallas_call(
        prepare_kernel,
        grid=(chunks,),
        out_shape=[
            jax.ShapeDtypeStruct((chunks, hidden, CHUNK), BF),
            jax.ShapeDtypeStruct((chunks, latent, CHUNK), BF),
            jax.ShapeDtypeStruct((chunks, nodes + slots, CHUNK), BF),
        ],
        in_specs=[rows, rows, index, index, whole(node_lat.shape), whole(w_edge_in_t.shape)],
        out_specs=[out(hidden), out(latent), out(nodes + slots)],
        scratch_shapes=[pltpu.VMEM((hidden, nodes), BF)],
        compiler_params=pltpu.CompilerParams(vmem_limit_bytes=VMEM_LIMIT),
        cost_estimate=pl.CostEstimate(
            flops=4 * edges * latent * hidden, bytes_accessed=8 * edges * latent, transcendentals=0
        ),
        name="prepare_edges",
    )(edge_lat, edge_cot, recv_rows, slot_rows, node_lat, w_edge_in_t)


def layer_kernel(
    piece_rows,
    core_ref,
    part_hbm,
    cot_hbm,
    hot_hbm,
    edge_hbm,
    valid_ref,
    fetched_ref,
    node_ref,
    node_cot_ref,
    w_in_ref,
    w_in_t_ref,
    w_out_ref,
    w_out_t_ref,
    gain_edge_ref,
    w_node_in_ref,
    w_node_in_t_ref,
    w_node_out_ref,
    w_node_out_t_ref,
    gain_node_ref,
    grad_pre_hbm,
    node_local_ref,
    pack_ref,
    part,
    cot,
    hot,
    edge,
    hidden,
    slope,
    normed,
    scale,
    grad_pre,
    send_part,
    summed_acc,
    w_in_acc,
    w_out_acc,
    ends_acc,
    gain_acc,
    grad_summed,
    weight_pack,
    sems,
    out_sems,
):
    chunks, latent, width = part.shape
    nodes = node_ref.shape[0]
    slots = fetched_ref.shape[0]
    bands = pack_ref.shape[1] * 2
    cap = slots // bands

    def incoming(c):
        return (
            pltpu.make_async_copy(part_hbm.at[c], part.at[c], sems.at[0, c]),
            pltpu.make_async_copy(hot_hbm.at[c], hot.at[c], sems.at[1, c]),
        )

    def incoming_later(c):
        return (
            pltpu.make_async_copy(cot_hbm.at[c], cot.at[c], sems.at[2, c]),
            pltpu.make_async_copy(edge_hbm.at[c], edge.at[c], sems.at[3, c]),
        )

    for c in range(chunks):
        for copy in incoming(c):
            copy.start()
    for c in range(chunks):
        for copy in incoming_later(c):
            copy.start()

    send_part[...] = dot(w_in_t_ref[:, latent : 2 * latent], fetched_ref[...], 1, 1).astype(BF)
    summed_acc[...] = jnp.zeros_like(summed_acc)
    w_in_acc[...] = jnp.zeros_like(w_in_acc)
    w_out_acc[...] = jnp.zeros_like(w_out_acc)
    ends_acc[...] = jnp.zeros_like(ends_acc)
    gain_acc[...] = jnp.zeros_like(gain_acc)

    @pl.loop(0, chunks)
    def _(c):
        for copy in incoming(c):
            copy.wait()
        pre = part[c].astype(F32) + dot(send_part[...], hot[c, nodes:, :], 1, 0)
        hid, slo = swish_and_slope(pre)
        hid = hid.astype(BF)
        hidden[c] = hid
        slope[c] = slo.astype(BF)
        out = dot(w_out_t_ref[...], hid, 1, 0)
        centred = out - jnp.mean(out, axis=0, keepdims=True)
        inv = lax.rsqrt(jnp.mean(centred * centred, axis=0, keepdims=True) + epsilon)
        inv = inv * valid_ref[c]
        scale[c] = inv
        norm = (centred * inv).astype(BF)
        normed[c] = norm
        summed_acc[...] += dot(norm, hot[c, :nodes, :], 1, 1)

    node = node_ref[...]
    summed = (summed_acc[...] * gain_edge_ref[...]).astype(BF)
    pre_node = dot(w_node_in_t_ref[:, :latent], node, 1, 1) + dot(
        w_node_in_t_ref[:, latent:], summed, 1, 0
    )
    hid_node, slope_node = swish_and_slope(pre_node)
    hid_node = hid_node.astype(BF)
    out_node = dot(w_node_out_t_ref[...], hid_node, 1, 0)
    centred = out_node - jnp.mean(out_node, axis=0, keepdims=True)
    inv_node = lax.rsqrt(jnp.mean(centred * centred, axis=0, keepdims=True) + epsilon)
    norm_node = centred * inv_node
    node_base = node_cot_ref[...].astype(F32)
    cot_node = node_base.T
    product = cot_node * norm_node
    gain_node_grad = jnp.sum(product.T, axis=0, keepdims=True)
    dy = cot_node * gain_node_ref[...]
    grad_out_node = (
        inv_node
        * (
            dy
            - jnp.mean(dy, axis=0, keepdims=True)
            - norm_node * jnp.mean(dy * norm_node, axis=0, keepdims=True)
        )
    ).astype(BF)
    base = 4 * latent
    weight_pack[base + 2 * latent : base + 3 * latent, :] = dot(hid_node, grad_out_node, 1, 1)
    grad_pre_node = (dot(w_node_out_ref[...], grad_out_node, 1, 0) * slope_node).astype(BF)
    weight_pack[base : base + latent, :] = dot(node, grad_pre_node, 0, 1)
    weight_pack[base + latent : base + 2 * latent, :] = dot(summed, grad_pre_node, 1, 1)
    grad_summed[...] = dot(w_node_in_ref[latent:, :], grad_pre_node, 1, 0).astype(BF)
    node_local = node_base + dot(grad_pre_node, w_node_in_ref[:latent, :], 0, 1)

    @pl.loop(0, chunks)
    def _(c):
        for copy in incoming_later(c):
            copy.wait()
        grad_update = cot[c].astype(F32) + dot(grad_summed[...], hot[c, :nodes, :], 1, 0)
        norm = normed[c].astype(F32)
        product = grad_update * norm
        gain_acc[...] += product
        gain = gain_edge_ref[...]
        dy = grad_update * gain
        mean_dy = jnp.mean(dy, axis=0, keepdims=True)
        mean_product = jnp.mean(product * gain, axis=0, keepdims=True)
        grad_out = (scale[c] * (dy - mean_dy - norm * mean_product)).astype(BF)
        w_out_acc[...] += dot(hidden[c], grad_out, 1, 1)
        grad_hidden = dot(w_out_ref[...], grad_out, 1, 0)
        grad_in = (grad_hidden * slope[c].astype(F32)).astype(BF)
        grad_pre[c] = grad_in
        pltpu.make_async_copy(grad_pre.at[c], grad_pre_hbm.at[c], out_sems.at[c]).start()
        w_in_acc[...] += dot(grad_in, edge[c], 1, 0)
        ends_acc[...] += dot(grad_in, hot[c], 1, 1)

    recv_sum = ends_acc[:, :nodes].astype(BF)
    slot_sum = ends_acc[:, nodes:].astype(BF)
    node_local_ref[...] = node_local + dot(recv_sum, w_in_ref[2 * latent :, :], 0, 1)
    weight_pack[:latent, :] = w_in_acc[...].T
    weight_pack[latent : 2 * latent, :] = dot(fetched_ref[...], slot_sum, 0, 1)
    weight_pack[2 * latent : 3 * latent, :] = dot(node, recv_sum, 0, 1)
    weight_pack[3 * latent : 4 * latent, :] = w_out_acc[...]
    tail = base + 3 * latent
    weight_pack[tail:, :] = jnp.zeros_like(weight_pack[tail:, :])
    weight_pack[tail : tail + 1, :] = jnp.sum(gain_acc[...].T, axis=0, keepdims=True)
    weight_pack[tail + 1 : tail + 2, :] = gain_node_grad
    slot_grads = dot(slot_sum, w_in_ref[latent : 2 * latent, :], 0, 1).astype(BF)
    core = core_ref[0]
    for d in range(bands):
        side = core if d % 2 == 0 else 1 - core
        pack_ref[side, d // 2, :cap, :] = slot_grads[d * cap : (d + 1) * cap, :]
        pack_ref[side, d // 2, cap:, :] = weight_pack[
            d * piece_rows : (d + 1) * piece_rows, :
        ].astype(BF)
    for c in range(chunks):
        pltpu.make_async_copy(grad_pre.at[c], grad_pre_hbm.at[c], out_sems.at[c]).wait()


def layer(core, part, cot_t, hot, edge_lat, valid_rows, fetched, node_lat, node_cot, weights, bands):
    chunks, hidden, width = part.shape
    nodes, latent = node_lat.shape
    slots = fetched.shape[0]
    cap = slots // bands
    used = 7 * latent + 2
    piece_rows = -(-used // (bands * 16)) * 16
    edge_chunks = edge_lat.reshape(chunks, width, latent)
    hbm = pl.BlockSpec(memory_space=pl.ANY)
    return pl.pallas_call(
        functools.partial(layer_kernel, piece_rows),
        out_shape=[
            jax.ShapeDtypeStruct((chunks, hidden, width), BF),
            jax.ShapeDtypeStruct((nodes, latent), F32),
            jax.ShapeDtypeStruct((2, bands // 2, cap + piece_rows, latent), BF),
        ],
        in_specs=[pl.BlockSpec(memory_space=pltpu.SMEM)] + [hbm] * 4 + [vmem()] * 14,
        out_specs=[hbm, vmem(), vmem()],
        scratch_shapes=[
            pltpu.VMEM((chunks, hidden, width), BF),
            pltpu.VMEM((chunks, latent, width), BF),
            pltpu.VMEM((chunks, nodes + slots, width), BF),
            pltpu.VMEM((chunks, width, latent), BF),
            pltpu.VMEM((chunks, hidden, width), BF),
            pltpu.VMEM((chunks, hidden, width), BF),
            pltpu.VMEM((chunks, latent, width), BF),
            pltpu.VMEM((chunks, 1, width), F32),
            pltpu.VMEM((chunks, hidden, width), BF),
            pltpu.VMEM((hidden, slots), BF),
            pltpu.VMEM((latent, nodes), F32),
            pltpu.VMEM((hidden, latent), F32),
            pltpu.VMEM((hidden, latent), F32),
            pltpu.VMEM((hidden, nodes + slots), F32),
            pltpu.VMEM((latent, width), F32),
            pltpu.VMEM((latent, nodes), BF),
            pltpu.VMEM((piece_rows * bands, latent), F32),
            pltpu.SemaphoreType.DMA((4, chunks)),
            pltpu.SemaphoreType.DMA((chunks,)),
        ],
        compiler_params=pltpu.CompilerParams(vmem_limit_bytes=VMEM_LIMIT),
        name="layer_backward",
    )(core, part, cot_t, hot, edge_chunks, valid_rows, fetched, node_lat, node_cot, *weights)


def edge_kernel(grad_ref, cot_ref, w_in_ref, out_ref):
    latent = cot_ref.shape[1]
    back = dot(grad_ref[0], w_in_ref[:latent, :], 0, 1)
    out_ref[...] = (cot_ref[...].astype(F32) + back).astype(BF)


def edge_result(grad_pre, edge_cot, w_edge_in):
    chunks, hidden, width = grad_pre.shape
    latent = edge_cot.shape[1]
    rows = pl.BlockSpec((width, latent), lambda i: (i, 0))
    return pl.pallas_call(
        edge_kernel,
        grid=(chunks,),
        out_shape=jax.ShapeDtypeStruct(edge_cot.shape, BF),
        in_specs=[
            pl.BlockSpec((1, hidden, width), lambda i: (i, 0, 0)),
            rows,
            whole(w_edge_in.shape),
        ],
        out_specs=rows,
        compiler_params=pltpu.CompilerParams(vmem_limit_bytes=VMEM_LIMIT),
        cost_estimate=pl.CostEstimate(
            flops=2 * chunks * width * hidden * latent,
            bytes_accessed=6 * chunks * width * latent,
            transcendentals=0,
        ),
        name="edge_result",
    )(grad_pre, edge_cot, w_edge_in)


def join_kernel(cap, pack_ref, got_ref, out_ref):
    out_ref[:, :cap, :] = pack_ref[:, :cap, :]
    out_ref[:, cap : 2 * cap, :] = got_ref[:, :cap, :]
    out_ref[:, 2 * cap :, :] = (
        pack_ref[:, cap:, :].astype(F32) + got_ref[:, cap:, :].astype(F32)
    ).astype(BF)


def join(keep, got, cap):
    chips, height, latent = keep.shape
    return pl.pallas_call(
        functools.partial(join_kernel, cap),
        out_shape=jax.ShapeDtypeStruct((chips, height + cap, latent), BF),
        in_specs=[vmem(), vmem()],
        out_specs=vmem(),
        name="join_cores",
    )(keep, got)


def settle_kernel(cap, asked_ref, back_ref, local_ref, node_grad_ref, piece_ref):
    chips, height, latent = back_ref.shape
    rows = back_ref[:, : 2 * cap, :].reshape(chips * 2 * cap, latent)
    picks = onehot_rows(local_ref.shape[0], asked_ref[...])
    node_grad_ref[...] = local_ref[...] + dot(picks, rows, 1, 0)
    piece_ref[...] = jnp.sum(back_ref[:, 2 * cap :, :].astype(F32), axis=0).astype(BF)


def settle(asked_row, back, node_local, cap):
    chips, height, latent = back.shape
    return pl.pallas_call(
        functools.partial(settle_kernel, cap),
        out_shape=[
            jax.ShapeDtypeStruct(node_local.shape, F32),
            jax.ShapeDtypeStruct((height - 2 * cap, latent), BF),
        ],
        in_specs=[vmem()] * 3,
        out_specs=[vmem()] * 2,
        name="settle_sums",
    )(asked_row, back, node_local)


def per_device(
    node_lat,
    edge_lat,
    node_cot,
    edge_cot,
    w_edge_in,
    w_edge_out,
    gain_edge,
    w_node_in,
    w_node_out,
    gain_node,
    fetch_idx,
    edge_slot,
    edge_recv,
    block_fill,
):
    bands = lax.axis_size("band")
    chips = bands // 2
    me = lax.axis_index("band")
    core = me % 2
    latent = node_lat.shape[1]
    cap = fetch_idx.shape[2]
    slots = bands * cap
    chunks = edge_lat.shape[0] // CHUNK
    other_core = [(i, i ^ 1) for i in range(bands)]
    same_core = [[2 * i + c for i in range(chips)] for c in range(2)]

    asked = lax.all_to_all(fetch_idx[0], "band", split_axis=0, concat_axis=0, tiled=True)
    rows = serve(asked.reshape(1, slots), node_lat)
    fetched = lax.all_to_all(
        rows.reshape(bands, cap, latent), "band", split_axis=0, concat_axis=0, tiled=True
    ).reshape(slots, latent)

    valid = jnp.arange(128, dtype=jnp.int32)[None, :] < block_fill[0][:, None]
    valid = valid.reshape(chunks, 1, CHUNK)
    recv_rows = edge_recv.reshape(chunks, 1, CHUNK)
    slot_rows = edge_slot.reshape(chunks, 1, CHUNK)
    part, cot_t, hot = prepare(
        edge_lat, edge_cot, recv_rows, slot_rows, node_lat, w_edge_in.T, slots
    )
    weights = (
        w_edge_in,
        w_edge_in.T,
        w_edge_out,
        w_edge_out.T,
        gain_edge[:, None],
        w_node_in,
        w_node_in.T,
        w_node_out,
        w_node_out.T,
        gain_node[:, None],
    )
    grad_pre, node_local, pack = layer(
        core.reshape(1).astype(jnp.int32),
        part,
        cot_t,
        hot,
        edge_lat,
        valid.astype(F32),
        fetched,
        node_lat,
        node_cot,
        weights,
        bands,
    )
    got = lax.ppermute(pack[1], "band", other_core)
    joined = join(pack[0], got, cap)
    back = lax.all_to_all(
        joined, "band", split_axis=0, concat_axis=0, tiled=True, axis_index_groups=same_core
    )
    edge_grad = edge_result(grad_pre, edge_cot, w_edge_in)
    asked_pairs = asked.reshape(chips, 2, cap)
    asked_pairs = jnp.where(core == 0, asked_pairs, asked_pairs[:, ::-1, :])
    node_grad, piece = settle(asked_pairs.reshape(1, slots), back, node_local, cap)
    mine = lax.all_to_all(
        jnp.broadcast_to(piece[None], (chips,) + piece.shape),
        "band",
        split_axis=0,
        concat_axis=0,
        tiled=True,
        axis_index_groups=same_core,
    )
    theirs = lax.ppermute(mine, "band", other_core)
    both = jnp.where(
        core == 0, jnp.stack([mine, theirs], axis=1), jnp.stack([theirs, mine], axis=1)
    ).reshape(-1, latent)
    both = both.astype(F32)
    return (
        node_grad,
        edge_grad,
        both[: 3 * latent],
        both[3 * latent : 4 * latent],
        both[7 * latent],
        both[4 * latent : 6 * latent],
        both[6 * latent : 7 * latent],
        both[7 * latent + 1],
    )


def solution(mesh):
    in_specs = (
        P(("grp", "band"), None),
        P(("grp", "band"), None),
        P(("grp", "band"), None),
        P(("grp", "band"), None),
        P(),
        P(),
        P(),
        P(),
        P(),
        P(),
        P("band", None, None),
        P("band"),
        P("band"),
        P("band", None),
    )
    out_specs = (
        P(("grp", "band"), None),
        P(("grp", "band"), None),
        P("grp", None),
        P("grp", None),
        P("grp"),
        P("grp", None),
        P("grp", None),
        P("grp"),
    )
    return jax.shard_map(
        per_device, mesh=mesh, in_specs=in_specs, out_specs=out_specs, check_vma=False
    )
```

```python
import functools

import jax
import jax.numpy as jnp
from jax import lax
from jax.experimental import pallas as pl
from jax.experimental.pallas import tpu as pltpu
from jax.sharding import PartitionSpec as P

epsilon = 1e-05
CHUNK = 512
VMEM_LIMIT = 60 * 2**20
BF = jnp.bfloat16
F32 = jnp.float32


def dot(lhs, rhs, lhs_dim, rhs_dim):
    return lax.dot_general(
        lhs, rhs, (((lhs_dim,), (rhs_dim,)), ((), ())), preferred_element_type=F32
    )


def swish_and_slope(values):
    logistic = jax.nn.sigmoid(values)
    hidden = values * logistic
    return hidden, logistic + hidden * (1.0 - logistic)


def onehot_rows(row_count, index_row):
    rows = lax.broadcasted_iota(jnp.int32, (row_count, index_row.shape[1]), 0)
    return (rows == index_row).astype(BF)


def vmem():
    return pl.BlockSpec(memory_space=pltpu.VMEM)


def whole(shape):
    return pl.BlockSpec(shape, lambda *_: (0,) * len(shape))


def serve_kernel(asked_ref, node_ref, rows_ref):
    cap = asked_ref.shape[1]
    node = node_ref[...]
    for d in range(asked_ref.shape[0]):
        picks = onehot_rows(node.shape[0], asked_ref[d : d + 1, :])
        rows_ref[d * cap : (d + 1) * cap, :] = dot(picks, node, 0, 0).astype(BF)


def serve(asked, node_lat):
    return pl.pallas_call(
        serve_kernel,
        out_shape=jax.ShapeDtypeStruct((asked.size, node_lat.shape[1]), BF),
        in_specs=[vmem(), vmem()],
        out_specs=vmem(),
        name="serve_rows",
    )(asked, node_lat)


def prepare_kernel(
    edge_ref,
    cot_ref,
    recv_ref,
    slot_ref,
    node_ref,
    w_in_ref,
    part_ref,
    cot_t_ref,
    hot_ref,
    node_part,
    w_edge_t,
):
    latent = edge_ref.shape[1]
    nodes = node_ref.shape[0]
    slots = hot_ref.shape[1] - nodes

    @pl.when(pl.program_id(0) == 0)
    def _():
        node_part[...] = dot(w_in_ref[2 * latent :, :], node_ref[...], 0, 1).astype(BF)
        w_edge_t[...] = w_in_ref[:latent, :].T

    recv_hot = onehot_rows(nodes, recv_ref[0])
    hot_ref[0, :nodes, :] = recv_hot
    hot_ref[0, nodes:, :] = onehot_rows(slots, slot_ref[0])
    part_ref[0] = dot(w_edge_t[...], edge_ref[...], 1, 1) + dot(node_part[...], recv_hot, 1, 0)
    cot_t_ref[0] = cot_ref[...].T


def prepare(edge_lat, edge_cot, recv_rows, slot_rows, node_lat, w_edge_in, slots):
    edges, latent = edge_lat.shape
    hidden = w_edge_in.shape[1]
    nodes = node_lat.shape[0]
    chunks = edges // CHUNK
    rows = pl.BlockSpec((CHUNK, latent), lambda i: (i, 0))
    index = pl.BlockSpec((1, 1, CHUNK), lambda i: (i, 0, 0))

    def out(height):
        return pl.BlockSpec((1, height, CHUNK), lambda i: (i, 0, 0))

    return pl.pallas_call(
        prepare_kernel,
        grid=(chunks,),
        out_shape=[
            jax.ShapeDtypeStruct((chunks, hidden, CHUNK), F32),
            jax.ShapeDtypeStruct((chunks, latent, CHUNK), BF),
            jax.ShapeDtypeStruct((chunks, nodes + slots, CHUNK), BF),
        ],
        in_specs=[rows, rows, index, index, whole(node_lat.shape), whole(w_edge_in.shape)],
        out_specs=[out(hidden), out(latent), out(nodes + slots)],
        scratch_shapes=[pltpu.VMEM((hidden, nodes), BF), pltpu.VMEM((hidden, latent), BF)],
        compiler_params=pltpu.CompilerParams(vmem_limit_bytes=VMEM_LIMIT),
        cost_estimate=pl.CostEstimate(
            flops=4 * edges * latent * hidden, bytes_accessed=8 * edges * latent, transcendentals=0
        ),
        name="prepare_edges",
    )(edge_lat, edge_cot, recv_rows, slot_rows, node_lat, w_edge_in)


def layer_kernel(
    piece_rows,
    core_ref,
    part_hbm,
    cot_hbm,
    hot_hbm,
    edge_hbm,
    valid_ref,
    fetched_ref,
    node_ref,
    node_cot_ref,
    w_in_ref,
    w_out_ref,
    gain_edge_ref,
    w_node_in_ref,
    w_node_out_ref,
    gain_node_ref,
    grad_pre_hbm,
    node_local_ref,
    keep_hbm,
    send_hbm,
    part,
    cot,
    hot,
    edge,
    hidden,
    slope,
    normed,
    scale,
    grad_pre,
    send_part,
    summed_acc,
    w_in_acc,
    w_out_acc,
    ends_acc,
    gain_acc,
    grad_summed,
    weight_pack,
    w_out_t,
    gain_column,
    pack,
    sems,
    out_sems,
    pack_sems,
):
    chunks, latent, width = part.shape
    nodes = node_ref.shape[0]
    slots = fetched_ref.shape[0]
    bands = pack.shape[1] * 2
    cap = slots // bands

    def incoming(c):
        return (
            pltpu.make_async_copy(part_hbm.at[c], part.at[c], sems.at[0, c]),
            pltpu.make_async_copy(hot_hbm.at[c], hot.at[c], sems.at[1, c]),
        )

    def incoming_later(c):
        return (
            pltpu.make_async_copy(cot_hbm.at[c], cot.at[c], sems.at[2, c]),
            pltpu.make_async_copy(edge_hbm.at[c], edge.at[c], sems.at[3, c]),
        )

    for c in range(chunks):
        for copy in incoming(c):
            copy.start()
    for c in range(chunks):
        for copy in incoming_later(c):
            copy.start()

    send_part[...] = dot(w_in_ref[latent : 2 * latent, :], fetched_ref[...], 0, 1).astype(BF)
    w_out_t[...] = w_out_ref[...].T
    gain_column[...] = jnp.broadcast_to(gain_edge_ref[...], (128, latent)).T
    summed_acc[...] = jnp.zeros_like(summed_acc)
    w_in_acc[...] = jnp.zeros_like(w_in_acc)
    w_out_acc[...] = jnp.zeros_like(w_out_acc)
    ends_acc[...] = jnp.zeros_like(ends_acc)
    gain_acc[...] = jnp.zeros_like(gain_acc)

    @pl.loop(0, chunks)
    def _(c):
        for copy in incoming(c):
            copy.wait()
        pre = part[c] + dot(send_part[...], hot[c, nodes:, :], 1, 0)
        hid, slo = swish_and_slope(pre)
        hid = hid.astype(BF)
        hidden[c] = hid
        slope[c] = slo.astype(BF)
        out = dot(w_out_t[...], hid, 1, 0)
        centred = out - jnp.mean(out, axis=0, keepdims=True)
        inv = lax.rsqrt(jnp.mean(centred * centred, axis=0, keepdims=True) + epsilon)
        inv = inv * valid_ref[c]
        scale[c] = inv
        norm = (centred * inv).astype(BF)
        normed[c] = norm
        summed_acc[...] += dot(norm, hot[c, :nodes, :], 1, 1)

    node = node_ref[...]
    summed = (summed_acc[...] * gain_column[:, :1]).astype(BF)
    pre_node = dot(w_node_in_ref[:latent, :], node, 0, 1) + dot(
        w_node_in_ref[latent:, :], summed, 0, 0
    )
    hid_node, slope_node = swish_and_slope(pre_node)
    hid_node = hid_node.astype(BF)
    out_node = dot(w_node_out_ref[...], hid_node, 0, 0)
    centred = out_node - jnp.mean(out_node, axis=0, keepdims=True)
    inv_node = lax.rsqrt(jnp.mean(centred * centred, axis=0, keepdims=True) + epsilon)
    norm_node = centred * inv_node
    node_base = node_cot_ref[...].astype(F32)
    cot_node = node_base.T
    product = cot_node * norm_node
    gain_node_grad = jnp.sum(product.T, axis=0, keepdims=True)
    dy = cot_node * jnp.broadcast_to(gain_node_ref[...], (128, latent)).T[:, :1]
    grad_out_node = (
        inv_node
        * (
            dy
            - jnp.mean(dy, axis=0, keepdims=True)
            - norm_node * jnp.mean(dy * norm_node, axis=0, keepdims=True)
        )
    ).astype(BF)
    base = 4 * latent
    weight_pack[base + 2 * latent : base + 3 * latent, :] = dot(hid_node, grad_out_node, 1, 1)
    grad_pre_node = (dot(w_node_out_ref[...], grad_out_node, 1, 0) * slope_node).astype(BF)
    weight_pack[base : base + latent, :] = dot(node, grad_pre_node, 0, 1)
    weight_pack[base + latent : base + 2 * latent, :] = dot(summed, grad_pre_node, 1, 1)
    grad_summed[...] = dot(w_node_in_ref[latent:, :], grad_pre_node, 1, 0).astype(BF)
    node_local = node_base + dot(grad_pre_node, w_node_in_ref[:latent, :], 0, 1)

    @pl.loop(0, chunks)
    def _(c):
        for copy in incoming_later(c):
            copy.wait()
        grad_update = cot[c].astype(F32) + dot(grad_summed[...], hot[c, :nodes, :], 1, 0)
        norm = normed[c].astype(F32)
        product = grad_update * norm
        gain_acc[...] += product
        gain = gain_column[:, :1]
        dy = grad_update * gain
        mean_dy = jnp.mean(dy, axis=0, keepdims=True)
        mean_product = jnp.mean(product * gain, axis=0, keepdims=True)
        grad_out = (scale[c] * (dy - mean_dy - norm * mean_product)).astype(BF)
        w_out_acc[...] += dot(hidden[c], grad_out, 1, 1)
        grad_hidden = dot(w_out_ref[...], grad_out, 1, 0)
        grad_in = (grad_hidden * slope[c].astype(F32)).astype(BF)
        grad_pre[c] = grad_in
        pltpu.make_async_copy(grad_pre.at[c], grad_pre_hbm.at[c], out_sems.at[c]).start()
        w_in_acc[...] += dot(grad_in, edge[c], 1, 0)
        ends_acc[...] += dot(grad_in, hot[c], 1, 1)

    recv_sum = ends_acc[:, :nodes].astype(BF)
    slot_sum = ends_acc[:, nodes:].astype(BF)
    node_local_ref[...] = node_local + dot(recv_sum, w_in_ref[2 * latent :, :], 0, 1)
    weight_pack[:latent, :] = w_in_acc[...].T
    weight_pack[latent : 2 * latent, :] = dot(fetched_ref[...], slot_sum, 0, 1)
    weight_pack[2 * latent : 3 * latent, :] = dot(node, recv_sum, 0, 1)
    weight_pack[3 * latent : 4 * latent, :] = w_out_acc[...]
    tail = base + 3 * latent
    weight_pack[tail:, :] = jnp.zeros_like(weight_pack[tail:, :])
    weight_pack[tail : tail + 1, :] = jnp.sum(gain_acc[...].T, axis=0, keepdims=True)
    weight_pack[tail + 1 : tail + 2, :] = gain_node_grad
    slot_grads = dot(slot_sum, w_in_ref[latent : 2 * latent, :], 0, 1).astype(BF)
    core = core_ref[0]
    for d in range(bands):
        pack[d % 2, d // 2, :cap, :] = slot_grads[d * cap : (d + 1) * cap, :]
        pack[d % 2, d // 2, cap:, :] = weight_pack[d * piece_rows : (d + 1) * piece_rows, :].astype(
            BF
        )
    for own in range(2):

        @pl.when(core == own)
        def _():
            keep = pltpu.make_async_copy(pack.at[own], keep_hbm, pack_sems.at[0])
            send = pltpu.make_async_copy(pack.at[1 - own], send_hbm, pack_sems.at[1])
            send.start()
            keep.start()
            send.wait()
            keep.wait()

    for c in range(chunks):
        pltpu.make_async_copy(grad_pre.at[c], grad_pre_hbm.at[c], out_sems.at[c]).wait()


def layer(core, part, cot_t, hot, edge_lat, valid_rows, fetched, node_lat, node_cot, weights, bands):
    chunks, hidden, width = part.shape
    nodes, latent = node_lat.shape
    slots = fetched.shape[0]
    cap = slots // bands
    used = 7 * latent + 2
    piece_rows = -(-used // (bands * 16)) * 16
    edge_chunks = edge_lat.reshape(chunks, width, latent)
    hbm = pl.BlockSpec(memory_space=pl.ANY)
    return pl.pallas_call(
        functools.partial(layer_kernel, piece_rows),
        out_shape=[
            jax.ShapeDtypeStruct((chunks, hidden, width), BF),
            jax.ShapeDtypeStruct((nodes, latent), F32),
            jax.ShapeDtypeStruct((bands // 2, cap + piece_rows, latent), BF),
            jax.ShapeDtypeStruct((bands // 2, cap + piece_rows, latent), BF),
        ],
        in_specs=[pl.BlockSpec(memory_space=pltpu.SMEM)] + [hbm] * 4 + [vmem()] * 10,
        out_specs=[hbm, vmem(), hbm, hbm],
        scratch_shapes=[
            pltpu.VMEM((chunks, hidden, width), F32),
            pltpu.VMEM((chunks, latent, width), BF),
            pltpu.VMEM((chunks, nodes + slots, width), BF),
            pltpu.VMEM((chunks, width, latent), BF),
            pltpu.VMEM((chunks, hidden, width), BF),
            pltpu.VMEM((chunks, hidden, width), BF),
            pltpu.VMEM((chunks, latent, width), BF),
            pltpu.VMEM((chunks, 1, width), F32),
            pltpu.VMEM((chunks, hidden, width), BF),
            pltpu.VMEM((hidden, slots), BF),
            pltpu.VMEM((latent, nodes), F32),
            pltpu.VMEM((hidden, latent), F32),
            pltpu.VMEM((hidden, latent), F32),
            pltpu.VMEM((hidden, nodes + slots), F32),
            pltpu.VMEM((latent, width), F32),
            pltpu.VMEM((latent, nodes), BF),
            pltpu.VMEM((piece_rows * bands, latent), F32),
            pltpu.VMEM((latent, hidden), BF),
            pltpu.VMEM((latent, 128), F32),
            pltpu.VMEM((2, bands // 2, cap + piece_rows, latent), BF),
            pltpu.SemaphoreType.DMA((4, chunks)),
            pltpu.SemaphoreType.DMA((chunks,)),
            pltpu.SemaphoreType.DMA((2,)),
        ],
        compiler_params=pltpu.CompilerParams(vmem_limit_bytes=VMEM_LIMIT),
        name="layer_backward",
    )(core, part, cot_t, hot, edge_chunks, valid_rows, fetched, node_lat, node_cot, *weights)


def edge_kernel(grad_ref, cot_ref, w_in_ref, out_ref):
    latent = cot_ref.shape[1]
    back = dot(grad_ref[0], w_in_ref[:latent, :], 0, 1)
    out_ref[...] = (cot_ref[...].astype(F32) + back).astype(BF)


def edge_result(grad_pre, edge_cot, w_edge_in):
    chunks, hidden, width = grad_pre.shape
    latent = edge_cot.shape[1]
    rows = pl.BlockSpec((width, latent), lambda i: (i, 0))
    return pl.pallas_call(
        edge_kernel,
        grid=(chunks,),
        out_shape=jax.ShapeDtypeStruct(edge_cot.shape, BF),
        in_specs=[
            pl.BlockSpec((1, hidden, width), lambda i: (i, 0, 0)),
            rows,
            whole(w_edge_in.shape),
        ],
        out_specs=rows,
        compiler_params=pltpu.CompilerParams(vmem_limit_bytes=VMEM_LIMIT),
        cost_estimate=pl.CostEstimate(
            flops=2 * chunks * width * hidden * latent,
            bytes_accessed=6 * chunks * width * latent,
            transcendentals=0,
        ),
        name="edge_result",
    )(grad_pre, edge_cot, w_edge_in)


def join_kernel(cap, pack_ref, got_ref, out_ref):
    out_ref[:, :cap, :] = pack_ref[:, :cap, :]
    out_ref[:, cap : 2 * cap, :] = got_ref[:, :cap, :]
    out_ref[:, 2 * cap :, :] = (
        pack_ref[:, cap:, :].astype(F32) + got_ref[:, cap:, :].astype(F32)
    ).astype(BF)


def join(keep, got, cap):
    chips, height, latent = keep.shape
    return pl.pallas_call(
        functools.partial(join_kernel, cap),
        out_shape=jax.ShapeDtypeStruct((chips, height + cap, latent), BF),
        in_specs=[vmem(), vmem()],
        out_specs=vmem(),
        name="join_cores",
    )(keep, got)


def settle_kernel(cap, core_ref, asked_ref, back_ref, local_ref, node_grad_ref, piece_ref):
    chips, height, latent = back_ref.shape
    rows = back_ref[:, : 2 * cap, :].reshape(chips * 2 * cap, latent)
    core = core_ref[0]
    lists = []
    for chip in range(chips):
        for turn in range(2):
            at = 2 * chip + (core if turn == 0 else 1 - core)
            lists.append(asked_ref[pl.ds(at, 1), :])
    picks = onehot_rows(local_ref.shape[0], jnp.concatenate(lists, axis=1))
    node_grad_ref[...] = local_ref[...] + dot(picks, rows, 1, 0)
    piece = jnp.sum(back_ref[:, 2 * cap :, :].astype(F32), axis=0).astype(BF)
    for chip in range(chips):
        piece_ref[chip] = piece


def settle(core, asked, back, node_local, cap):
    chips, height, latent = back.shape
    return pl.pallas_call(
        functools.partial(settle_kernel, cap),
        out_shape=[
            jax.ShapeDtypeStruct(node_local.shape, F32),
            jax.ShapeDtypeStruct((chips, height - 2 * cap, latent), BF),
        ],
        in_specs=[pl.BlockSpec(memory_space=pltpu.SMEM)] + [vmem()] * 3,
        out_specs=[vmem()] * 2,
        name="settle_sums",
    )(core, asked, back, node_local)


def assemble_kernel(core_ref, mine_ref, theirs_ref, *refs):
    outs, rows = refs[:-1], refs[-1]
    chips, height, latent = mine_ref.shape
    core = core_ref[0]
    for chip in range(chips):
        for ref, side in ((mine_ref, core), (theirs_ref, 1 - core)):
            start = pl.multiple_of((2 * chip + side) * height, height)
            rows[pl.ds(start, height), :] = ref[chip].astype(F32)
    at = 0
    for out in outs:
        out[...] = rows[at : at + out.shape[0], :]
        at += out.shape[0]


def assemble(core, mine, theirs, latent):
    chips, height, width = mine.shape
    heights = (3 * latent, latent, 2 * latent, latent, 1, 1)
    return pl.pallas_call(
        assemble_kernel,
        out_shape=[jax.ShapeDtypeStruct((rows, width), F32) for rows in heights],
        in_specs=[pl.BlockSpec(memory_space=pltpu.SMEM), vmem(), vmem()],
        out_specs=[vmem()] * len(heights),
        scratch_shapes=[pltpu.VMEM((2 * chips * height, width), F32)],
        name="assemble_sums",
    )(core, mine, theirs)


def per_device(
    node_lat,
    edge_lat,
    node_cot,
    edge_cot,
    w_edge_in,
    w_edge_out,
    gain_edge,
    w_node_in,
    w_node_out,
    gain_node,
    fetch_idx,
    edge_slot,
    edge_recv,
    block_fill,
):
    bands = lax.axis_size("band")
    chips = bands // 2
    me = lax.axis_index("band")
    core = (me % 2).reshape(1).astype(jnp.int32)
    latent = node_lat.shape[1]
    cap = fetch_idx.shape[2]
    slots = bands * cap
    chunks = edge_lat.shape[0] // CHUNK
    other_core = [(i, i ^ 1) for i in range(bands)]
    same_core = [[2 * i + c for i in range(chips)] for c in range(2)]

    asked = lax.all_to_all(fetch_idx[0], "band", split_axis=0, concat_axis=0, tiled=True)
    rows = serve(asked, node_lat)
    fetched = lax.all_to_all(
        rows.reshape(bands, cap, latent), "band", split_axis=0, concat_axis=0, tiled=True
    ).reshape(slots, latent)

    valid = jnp.arange(128, dtype=jnp.int32)[None, :] < block_fill[0][:, None]
    valid = valid.reshape(chunks, 1, CHUNK)
    recv_rows = edge_recv.reshape(chunks, 1, CHUNK)
    slot_rows = edge_slot.reshape(chunks, 1, CHUNK)
    part, cot_t, hot = prepare(
        edge_lat, edge_cot, recv_rows, slot_rows, node_lat, w_edge_in, slots
    )
    weights = (
        w_edge_in,
        w_edge_out,
        gain_edge[None, :],
        w_node_in,
        w_node_out,
        gain_node[None, :],
    )
    grad_pre, node_local, keep, send = layer(
        core,
        part,
        cot_t,
        hot,
        edge_lat,
        valid.astype(F32),
        fetched,
        node_lat,
        node_cot,
        weights,
        bands,
    )
    got = lax.ppermute(send, "band", other_core)
    joined = join(keep, got, cap)
    back = lax.all_to_all(
        joined, "band", split_axis=0, concat_axis=0, tiled=True, axis_index_groups=same_core
    )
    edge_grad = edge_result(grad_pre, edge_cot, w_edge_in)
    back, edge_grad = lax.optimization_barrier((back, edge_grad))
    node_grad, piece = settle(core, asked, back, node_local, cap)
    mine = lax.all_to_all(
        piece, "band", split_axis=0, concat_axis=0, tiled=True, axis_index_groups=same_core
    )
    theirs = lax.ppermute(mine, "band", other_core)
    sums = assemble(core, mine, theirs, latent)
    return (
        node_grad,
        edge_grad,
        sums[0],
        sums[1],
        sums[4].reshape(-1),
        sums[2],
        sums[3],
        sums[5].reshape(-1),
    )


def solution(mesh):
    in_specs = (
        P(("grp", "band"), None),
        P(("grp", "band"), None),
        P(("grp", "band"), None),
        P(("grp", "band"), None),
        P(),
        P(),
        P(),
        P(),
        P(),
        P(),
        P("band", None, None),
        P("band"),
        P("band"),
        P("band", None),
    )
    out_specs = (
        P(("grp", "band"), None),
        P(("grp", "band"), None),
        P("grp", None),
        P("grp", None),
        P("grp"),
        P("grp", None),
        P("grp", None),
        P("grp"),
    )
    return jax.shard_map(
        per_device, mesh=mesh, in_specs=in_specs, out_specs=out_specs, check_vma=False
    )
```

```python
import functools

import jax
import jax.numpy as jnp
from jax import lax
from jax.experimental import pallas as pl
from jax.experimental.pallas import tpu as pltpu
from jax.sharding import PartitionSpec as P

epsilon = 1e-05
CHUNK = 1280
GROUP = 4
TAIL = 16
VMEM_LIMIT = 60 * 2**20
BF = jnp.bfloat16
F32 = jnp.float32


def dot(lhs, rhs, lhs_dim, rhs_dim):
    return lax.dot_general(
        lhs, rhs, (((lhs_dim,), (rhs_dim,)), ((), ())), preferred_element_type=F32
    )


def swish_and_slope(values):
    logistic = jax.nn.sigmoid(values)
    hidden = values * logistic
    return hidden, logistic + hidden * (1.0 - logistic)


def onehot_rows(row_count, index_row):
    rows = lax.broadcasted_iota(jnp.int16, (row_count, index_row.shape[1]), 0)
    return jnp.where(rows == index_row.astype(jnp.int16), jnp.ones((), BF), jnp.zeros((), BF))


def vmem():
    return pl.BlockSpec(memory_space=pltpu.VMEM)


def whole(shape):
    return pl.BlockSpec(shape, lambda *_: (0,) * len(shape))


def serve_kernel(place_ref, lists_ref, *refs):
    members, rows_ref = refs[:-1], refs[-1]
    groups, _, cap = lists_ref.shape
    group, member = place_ref[1], place_ref[2] % GROUP
    for k, nodes_ref in enumerate(members):
        owner = member ^ k
        wanted = jnp.concatenate(
            [lists_ref[j, pl.ds(group * GROUP + owner, 1), :] for j in range(groups)], axis=1
        )
        picks = onehot_rows(nodes_ref.shape[0], wanted)
        rows = dot(picks, nodes_ref[...], 0, 0).astype(BF)
        place = pl.ds(pl.multiple_of(owner * cap, cap), cap)
        for j in range(groups):
            rows_ref[group ^ j, place, :] = rows[j * cap : (j + 1) * cap]


def serve(place, lists, members):
    groups, _, cap = lists.shape
    return pl.pallas_call(
        serve_kernel,
        out_shape=jax.ShapeDtypeStruct((groups, GROUP * cap, members[0].shape[1]), BF),
        in_specs=[pl.BlockSpec(memory_space=pltpu.SMEM)] + [vmem()] * (1 + GROUP),
        out_specs=vmem(),
        compiler_params=pltpu.CompilerParams(vmem_limit_bytes=VMEM_LIMIT),
        name="serve_rows",
    )(place, lists, *members)


def prepare_kernel(
    edge_ref, cot_ref, recv_ref, node_ref, w_in_ref, part_ref, cot_t_ref, node_part, w_edge_t
):
    latent = edge_ref.shape[1]

    @pl.when(pl.program_id(0) == 0)
    def _():
        node_part[...] = dot(w_in_ref[2 * latent :, :], node_ref[...], 0, 1).astype(BF)
        w_edge_t[...] = w_in_ref[:latent, :].T

    recv_hot = onehot_rows(node_ref.shape[0], recv_ref[0])
    part_ref[0] = dot(w_edge_t[...], edge_ref[...], 1, 1) + dot(node_part[...], recv_hot, 1, 0)
    cot_t_ref[0] = cot_ref[...].T


def prepare(edge_lat, edge_cot, recv_rows, node_lat, w_edge_in):
    edges, latent = edge_lat.shape
    hidden = w_edge_in.shape[1]
    nodes = node_lat.shape[0]
    chunks = edges // CHUNK
    rows = pl.BlockSpec((CHUNK, latent), lambda i: (i, 0))

    def along(height):
        return pl.BlockSpec((1, height, CHUNK), lambda i: (i, 0, 0))

    return pl.pallas_call(
        prepare_kernel,
        grid=(chunks,),
        out_shape=[
            jax.ShapeDtypeStruct((chunks, hidden, CHUNK), F32),
            jax.ShapeDtypeStruct((chunks, latent, CHUNK), BF),
        ],
        in_specs=[rows, rows, along(1), whole(node_lat.shape), whole(w_edge_in.shape)],
        out_specs=[along(hidden), along(latent)],
        scratch_shapes=[pltpu.VMEM((hidden, nodes), BF), pltpu.VMEM((hidden, latent), BF)],
        compiler_params=pltpu.CompilerParams(vmem_limit_bytes=VMEM_LIMIT),
        cost_estimate=pl.CostEstimate(
            flops=4 * edges * latent * hidden, bytes_accessed=8 * edges * latent, transcendentals=0
        ),
        name="prepare_edges",
    )(edge_lat, edge_cot, recv_rows, node_lat, w_edge_in)


def layer_kernel(
    piece_rows,
    core_ref,
    part_hbm,
    cot_hbm,
    edge_hbm,
    recv_ref,
    slot_ref,
    wanted_ref,
    valid_ref,
    fetched_ref,
    node_ref,
    node_cot_ref,
    w_in_ref,
    w_out_ref,
    gain_edge_ref,
    w_node_in_ref,
    w_node_out_ref,
    gain_node_ref,
    grad_pre_hbm,
    node_local_ref,
    keep_hbm,
    send_hbm,
    part,
    cot,
    edge,
    hot,
    hidden,
    slope,
    normed,
    scale,
    grad_pre,
    send_part,
    summed_acc,
    w_in_acc,
    w_out_acc,
    ends_acc,
    gain_acc,
    grad_summed,
    weight_pack,
    w_out_t,
    gain_column,
    pack,
    sems,
    out_sems,
    pack_sems,
):
    chunks, latent, width = part.shape
    nodes = node_ref.shape[0]
    slots = fetched_ref.shape[0]
    bands = pack.shape[1] * 2
    cap = slots // bands

    def part_copy(c):
        return pltpu.make_async_copy(part_hbm.at[c], part.at[c], sems.at[0, c])

    def cot_copy(c):
        return pltpu.make_async_copy(cot_hbm.at[c], cot.at[c], sems.at[1, c])

    def edge_copy(c):
        return pltpu.make_async_copy(edge_hbm.at[c], edge.at[c], sems.at[2, c])

    for copy in (part_copy, cot_copy, edge_copy):
        for c in range(chunks):
            copy(c).start()

    send_part[...] = dot(w_in_ref[latent : 2 * latent, :], fetched_ref[...], 0, 1).astype(BF)
    w_out_t[...] = w_out_ref[...].T
    gain_column[...] = jnp.broadcast_to(gain_edge_ref[...], (128, latent)).T
    summed_acc[...] = jnp.zeros_like(summed_acc)
    for c in range(chunks):
        part_copy(c).wait()
    w_in_acc[...] = jnp.zeros_like(w_in_acc)
    w_out_acc[...] = jnp.zeros_like(w_out_acc)
    ends_acc[...] = jnp.zeros_like(ends_acc)
    gain_acc[...] = jnp.zeros_like(gain_acc)

    @pl.loop(0, chunks, unroll=True)
    def _(c):
        slot_hot = onehot_rows(slots, slot_ref[c])
        recv_hot = onehot_rows(nodes, recv_ref[c])
        hot[c, :nodes, :] = recv_hot
        hot[c, nodes:, :] = slot_hot
        pre = part[c] + dot(send_part[...], slot_hot, 1, 0)
        hid, slo = swish_and_slope(pre)
        hid = hid.astype(BF)
        hidden[c] = hid
        slope[c] = slo.astype(BF)
        out = dot(w_out_t[...], hid, 1, 0)
        centred = out - jnp.mean(out, axis=0, keepdims=True)
        inv = lax.rsqrt(jnp.mean(centred * centred, axis=0, keepdims=True) + epsilon)
        inv = inv * valid_ref[c]
        scale[c] = inv
        norm = (centred * inv).astype(BF)
        normed[c] = norm
        summed_acc[...] += dot(norm, recv_hot, 1, 1)

    for c in range(chunks):
        cot_copy(c).wait()
        edge_copy(c).wait()
    node = node_ref[...]
    summed = (summed_acc[...] * gain_column[:, :1]).astype(BF)
    pre_node = dot(w_node_in_ref[:latent, :], node, 0, 1) + dot(
        w_node_in_ref[latent:, :], summed, 0, 0
    )
    hid_node, slope_node = swish_and_slope(pre_node)
    hid_node = hid_node.astype(BF)
    out_node = dot(w_node_out_ref[...], hid_node, 0, 0)
    centred = out_node - jnp.mean(out_node, axis=0, keepdims=True)
    inv_node = lax.rsqrt(jnp.mean(centred * centred, axis=0, keepdims=True) + epsilon)
    norm_node = centred * inv_node
    node_base = node_cot_ref[...].astype(F32)
    cot_node = node_base.T
    product = cot_node * norm_node
    gain_node_grad = jnp.sum(product.T, axis=0, keepdims=True)
    dy = cot_node * jnp.broadcast_to(gain_node_ref[...], (128, latent)).T[:, :1]
    grad_out_node = (
        inv_node
        * (
            dy
            - jnp.mean(dy, axis=0, keepdims=True)
            - norm_node * jnp.mean(dy * norm_node, axis=0, keepdims=True)
        )
    ).astype(BF)
    base = 4 * latent
    weight_pack[base + 2 * latent : base + 3 * latent, :] = dot(hid_node, grad_out_node, 1, 1)
    grad_pre_node = (dot(w_node_out_ref[...], grad_out_node, 1, 0) * slope_node).astype(BF)
    weight_pack[base : base + latent, :] = dot(node, grad_pre_node, 0, 1)
    weight_pack[base + latent : base + 2 * latent, :] = dot(summed, grad_pre_node, 1, 1)
    grad_summed[...] = dot(w_node_in_ref[latent:, :], grad_pre_node, 1, 0).astype(BF)
    node_local = node_base + dot(grad_pre_node, w_node_in_ref[:latent, :], 0, 1)

    @pl.loop(0, chunks, unroll=True)
    def _(c):
        grad_update = cot[c].astype(F32) + dot(grad_summed[...], hot[c, :nodes, :], 1, 0)
        norm = normed[c].astype(F32)
        product = grad_update * norm
        gain_acc[...] += product
        gain = gain_column[:, :1]
        dy = grad_update * gain
        mean_dy = jnp.mean(dy, axis=0, keepdims=True)
        mean_product = jnp.mean(product * gain, axis=0, keepdims=True)
        grad_out = (scale[c] * (dy - mean_dy - norm * mean_product)).astype(BF)
        w_out_acc[...] += dot(hidden[c], grad_out, 1, 1)
        grad_hidden = dot(w_out_ref[...], grad_out, 1, 0)
        grad_in = (grad_hidden * slope[c].astype(F32)).astype(BF)
        grad_pre[c] = grad_in
        w_in_acc[...] += dot(grad_in, edge[c], 1, 0)
        ends_acc[...] += dot(hot[c], grad_in, 1, 1)

    for c in range(chunks):
        pltpu.make_async_copy(grad_pre.at[c], grad_pre_hbm.at[c], out_sems.at[c]).start()
    recv_sum = ends_acc[:nodes, :].astype(BF)
    slot_sum = ends_acc[nodes:, :].astype(BF)
    node_local_ref[...] = node_local + dot(recv_sum, w_in_ref[2 * latent :, :], 1, 1)
    weight_pack[:latent, :] = w_in_acc[...].T
    weight_pack[latent : 2 * latent, :] = dot(fetched_ref[...], slot_sum, 0, 0)
    weight_pack[2 * latent : 3 * latent, :] = dot(node, recv_sum, 0, 0)
    weight_pack[3 * latent : 4 * latent, :] = w_out_acc[...]
    used = base + 3 * latent
    if used < weight_pack.shape[0]:
        weight_pack[used:, :] = jnp.zeros_like(weight_pack[used:, :])
    gain_edge_grad = jnp.sum(gain_acc[...].T, axis=0, keepdims=True)
    slot_grads = dot(slot_sum, w_in_ref[latent : 2 * latent, :], 1, 1).astype(BF)
    core = core_ref[0]
    for d in range(bands):
        pack[d % 2, d // 2, :cap, :] = slot_grads[d * cap : (d + 1) * cap, :]
        body = weight_pack[d * piece_rows : (d + 1) * piece_rows, :]
        pack[d % 2, d // 2, cap : cap + piece_rows, :] = body.astype(BF)
        row = lax.broadcasted_iota(jnp.int32, (TAIL, latent), 0)
        listed = jnp.concatenate([wanted_ref[d : d + 1, :].astype(F32)] * (latent // cap), axis=1)
        column = lax.broadcasted_iota(jnp.int32, (1, latent), 1)
        listed = jnp.where(column // cap == core, listed, 0.0)
        extra = jnp.where(row == 1, listed, 0.0)
        if d < 2:
            extra = jnp.where(row == 0, gain_edge_grad if d == 0 else gain_node_grad, extra)
        pack[d % 2, d // 2, cap + piece_rows :, :] = extra.astype(BF)
    for own in range(2):

        @pl.when(core == own)
        def _():
            keep = pltpu.make_async_copy(pack.at[own], keep_hbm, pack_sems.at[0])
            send = pltpu.make_async_copy(pack.at[1 - own], send_hbm, pack_sems.at[1])
            send.start()
            keep.start()
            send.wait()
            keep.wait()

    for c in range(chunks):
        pltpu.make_async_copy(grad_pre.at[c], grad_pre_hbm.at[c], out_sems.at[c]).wait()


def layer(
    core, part, cot_t, edge_lat, recv_rows, slot_rows, wanted, valid_rows, fetched, node_lat, node_cot, weights, bands
):
    chunks, hidden, width = part.shape
    edges = edge_lat.reshape(chunks, width, -1)
    nodes, latent = node_lat.shape
    slots = fetched.shape[0]
    cap = slots // bands
    piece_rows = -(-7 * latent // (bands * 16)) * 16
    hbm = pl.BlockSpec(memory_space=pl.ANY)
    return pl.pallas_call(
        functools.partial(layer_kernel, piece_rows),
        out_shape=[
            jax.ShapeDtypeStruct((chunks, hidden, width), BF),
            jax.ShapeDtypeStruct((nodes, latent), F32),
            jax.ShapeDtypeStruct((bands // 2, cap + piece_rows + TAIL, latent), BF),
            jax.ShapeDtypeStruct((bands // 2, cap + piece_rows + TAIL, latent), BF),
        ],
        in_specs=[pl.BlockSpec(memory_space=pltpu.SMEM)] + [hbm] * 3 + [vmem()] * 13,
        out_specs=[hbm, vmem(), hbm, hbm],
        scratch_shapes=[
            pltpu.VMEM((chunks, hidden, width), F32),
            pltpu.VMEM((chunks, latent, width), BF),
            pltpu.VMEM((chunks, width, latent), BF),
            pltpu.VMEM((chunks, nodes + slots, width), BF),
            pltpu.VMEM((chunks, hidden, width), BF),
            pltpu.VMEM((chunks, hidden, width), BF),
            pltpu.VMEM((chunks, latent, width), BF),
            pltpu.VMEM((chunks, 1, width), F32),
            pltpu.VMEM((chunks, hidden, width), BF),
            pltpu.VMEM((hidden, slots), BF),
            pltpu.VMEM((latent, nodes), F32),
            pltpu.VMEM((hidden, latent), F32),
            pltpu.VMEM((hidden, latent), F32),
            pltpu.VMEM((nodes + slots, hidden), F32),
            pltpu.VMEM((latent, width), F32),
            pltpu.VMEM((latent, nodes), BF),
            pltpu.VMEM((piece_rows * bands, latent), F32),
            pltpu.VMEM((latent, hidden), BF),
            pltpu.VMEM((latent, 128), F32),
            pltpu.VMEM((2, bands // 2, cap + piece_rows + TAIL, latent), BF),
            pltpu.SemaphoreType.DMA((3, chunks)),
            pltpu.SemaphoreType.DMA((chunks,)),
            pltpu.SemaphoreType.DMA((2,)),
        ],
        compiler_params=pltpu.CompilerParams(vmem_limit_bytes=VMEM_LIMIT),
        name="layer_backward",
    )(core, part, cot_t, edges, recv_rows, slot_rows, wanted, valid_rows, fetched, node_lat, node_cot, *weights)


def edge_kernel(grad_ref, cot_ref, w_in_ref, out_ref):
    latent = cot_ref.shape[1]
    back = dot(grad_ref[0], w_in_ref[:latent, :], 0, 1)
    out_ref[...] = (cot_ref[...].astype(F32) + back).astype(BF)


def edge_result(grad_pre, edge_cot, w_edge_in):
    chunks, hidden, width = grad_pre.shape
    latent = edge_cot.shape[1]
    rows = pl.BlockSpec((width, latent), lambda i: (i, 0))
    return pl.pallas_call(
        edge_kernel,
        grid=(chunks,),
        out_shape=jax.ShapeDtypeStruct(edge_cot.shape, BF),
        in_specs=[
            pl.BlockSpec((1, hidden, width), lambda i: (i, 0, 0)),
            rows,
            whole(w_edge_in.shape),
        ],
        out_specs=rows,
        compiler_params=pltpu.CompilerParams(vmem_limit_bytes=VMEM_LIMIT),
        cost_estimate=pl.CostEstimate(
            flops=2 * chunks * width * hidden * latent,
            bytes_accessed=6 * chunks * width * latent,
            transcendentals=0,
        ),
        name="edge_result",
    )(grad_pre, edge_cot, w_edge_in)


def join_kernel(cap, pack_ref, got_ref, out_ref):
    out_ref[:, :cap, :] = pack_ref[:, :cap, :]
    out_ref[:, cap : 2 * cap, :] = got_ref[:, :cap, :]
    out_ref[:, 2 * cap :, :] = (
        pack_ref[:, cap:, :].astype(F32) + got_ref[:, cap:, :].astype(F32)
    ).astype(BF)


def join(keep, got, cap):
    chips, height, latent = keep.shape
    return pl.pallas_call(
        functools.partial(join_kernel, cap),
        out_shape=jax.ShapeDtypeStruct((chips, height + cap, latent), BF),
        in_specs=[vmem(), vmem()],
        out_specs=vmem(),
        name="join_cores",
    )(keep, got)


def settle_kernel(cap, core_ref, back_ref, local_ref, node_grad_ref, piece_ref):
    chips, height, latent = back_ref.shape
    rows = back_ref[:, : 2 * cap, :].reshape(chips * 2 * cap, latent)
    core = core_ref[0]
    listed = back_ref[:, height - TAIL + 1, :].astype(F32)
    lists = []
    for chip in range(chips):
        first, second = listed[chip : chip + 1, :cap], listed[chip : chip + 1, cap : 2 * cap]
        lists.append(jnp.where(core == 0, first, second))
        lists.append(jnp.where(core == 0, second, first))
    picks = onehot_rows(local_ref.shape[0], jnp.concatenate(lists, axis=1).astype(jnp.int32))
    node_grad_ref[...] = local_ref[...] + dot(picks, rows, 1, 0)
    piece = jnp.sum(back_ref[:, 2 * cap :, :].astype(F32), axis=0).astype(BF)
    for chip in range(chips):
        piece_ref[chip] = piece


def settle(place, back, node_local, cap):
    chips, height, latent = back.shape
    return pl.pallas_call(
        functools.partial(settle_kernel, cap),
        out_shape=[
            jax.ShapeDtypeStruct(node_local.shape, F32),
            jax.ShapeDtypeStruct((chips, height - 2 * cap, latent), BF),
        ],
        in_specs=[pl.BlockSpec(memory_space=pltpu.SMEM)] + [vmem()] * 2,
        out_specs=[vmem()] * 2,
        name="settle_sums",
    )(place, back, node_local)


def assemble_kernel(core_ref, mine_ref, theirs_ref, *refs):
    outs, rows = refs[:-1], refs[-1]
    chips, height, latent = mine_ref.shape
    body = height - TAIL
    core = core_ref[0]
    for chip in range(chips):
        for ref, side in ((mine_ref, core), (theirs_ref, 1 - core)):
            start = pl.multiple_of((2 * chip + side) * body, body)
            rows[pl.ds(start, body), :] = ref[chip, :body, :].astype(F32)
    first, second = mine_ref[0, body:, :].astype(F32), theirs_ref[0, body:, :].astype(F32)
    outs[-2][...] = jnp.where(core == 0, first, second)[:1]
    outs[-1][...] = jnp.where(core == 0, second, first)[:1]
    at = 0
    for out in outs[:-2]:
        out[...] = rows[at : at + out.shape[0], :]
        at += out.shape[0]


def assemble(place, mine, theirs, latent):
    chips, height, width = mine.shape
    heights = (3 * latent, latent, 2 * latent, latent, 1, 1)
    return pl.pallas_call(
        assemble_kernel,
        out_shape=[jax.ShapeDtypeStruct((rows, width), F32) for rows in heights],
        in_specs=[pl.BlockSpec(memory_space=pltpu.SMEM), vmem(), vmem()],
        out_specs=[vmem()] * len(heights),
        scratch_shapes=[pltpu.VMEM((2 * chips * (height - TAIL), width), F32)],
        name="assemble_sums",
    )(place, mine, theirs)


def per_device(
    node_lat,
    edge_lat,
    node_cot,
    edge_cot,
    w_edge_in,
    w_edge_out,
    gain_edge,
    w_node_in,
    w_node_out,
    gain_node,
    fetch_idx,
    edge_slot,
    edge_recv,
    block_fill,
):
    bands = lax.axis_size("band")
    chips = bands // 2
    me = lax.axis_index("band")
    place = jnp.stack([me % 2, me // GROUP, me]).astype(jnp.int32)
    latent = node_lat.shape[1]
    cap = fetch_idx.shape[2]
    slots = bands * cap
    chunks = edge_lat.shape[0] // CHUNK
    other_core = [(i, i ^ 1) for i in range(bands)]
    same_core = [[2 * i + c for i in range(chips)] for c in range(2)]

    groups = bands // GROUP
    like_placed = [[GROUP * g + i for g in range(groups)] for i in range(GROUP)]

    def swap(array, step):
        return lax.ppermute(array, "band", [(i, i ^ step) for i in range(bands)])

    across = swap(node_lat, 2)
    lists = fetch_idx
    step = GROUP
    while step < bands:
        lists = jnp.concatenate([lists, swap(lists, step)], axis=0)
        step *= 2
    members = (node_lat, swap(node_lat, 1), across, swap(across, 1))
    rows = serve(place, lists, members)
    valid = jnp.arange(128, dtype=jnp.int32)[None, :] < block_fill[0][:, None]
    valid = valid.astype(F32).reshape(chunks, 1, CHUNK)
    recv_rows = edge_recv.reshape(chunks, 1, CHUNK)
    recv_rows, rows = lax.optimization_barrier((recv_rows, rows))
    fetched = lax.all_to_all(
        rows, "band", split_axis=0, concat_axis=0, tiled=True, axis_index_groups=like_placed
    ).reshape(slots, latent)

    slot_rows = edge_slot.reshape(chunks, 1, CHUNK)
    part, cot_t = prepare(
        edge_lat, edge_cot, recv_rows, node_lat, w_edge_in
    )
    weights = (
        w_edge_in,
        w_edge_out,
        gain_edge[None, :],
        w_node_in,
        w_node_out,
        gain_node[None, :],
    )
    grad_pre, node_local, keep, send = layer(
        place,
        part,
        cot_t,
        edge_lat,
        recv_rows,
        slot_rows,
        fetch_idx[0],
        valid,
        fetched,
        node_lat,
        node_cot,
        weights,
        bands,
    )
    got = lax.ppermute(send, "band", other_core)
    joined = join(keep, got, cap)
    back = lax.all_to_all(
        joined, "band", split_axis=0, concat_axis=0, tiled=True, axis_index_groups=same_core
    )
    edge_grad = edge_result(grad_pre, edge_cot, w_edge_in)
    back, edge_grad = lax.optimization_barrier((back, edge_grad))
    node_grad, piece = settle(place, back, node_local, cap)
    mine = lax.all_to_all(
        piece, "band", split_axis=0, concat_axis=0, tiled=True, axis_index_groups=same_core
    )
    theirs = lax.ppermute(mine, "band", other_core)
    sums = assemble(place, mine, theirs, latent)
    return (
        node_grad,
        edge_grad,
        sums[0],
        sums[1],
        sums[4].reshape(-1),
        sums[2],
        sums[3],
        sums[5].reshape(-1),
    )


def solution(mesh):
    in_specs = (
        P(("grp", "band"), None),
        P(("grp", "band"), None),
        P(("grp", "band"), None),
        P(("grp", "band"), None),
        P(),
        P(),
        P(),
        P(),
        P(),
        P(),
        P("band", None, None),
        P("band"),
        P("band"),
        P("band", None),
    )
    out_specs = (
        P(("grp", "band"), None),
        P(("grp", "band"), None),
        P("grp", None),
        P("grp", None),
        P("grp"),
        P("grp", None),
        P("grp", None),
        P("grp"),
    )
    return jax.shard_map(
        per_device, mesh=mesh, in_specs=in_specs, out_specs=out_specs, check_vma=False
    )
```

```python
import functools

import jax
import jax.numpy as jnp
from jax import lax
from jax.experimental import pallas as pl
from jax.experimental.pallas import tpu as pltpu
from jax.sharding import PartitionSpec as P

epsilon = 1e-05
CHUNK = 1280
GROUP = 4
TAIL = 16
VMEM_LIMIT = 60 * 2**20
BF = jnp.bfloat16
F32 = jnp.float32


def dot(lhs, rhs, lhs_dim, rhs_dim):
    return lax.dot_general(
        lhs, rhs, (((lhs_dim,), (rhs_dim,)), ((), ())), preferred_element_type=F32
    )


def swish_and_slope(values):
    logistic = jax.nn.sigmoid(values)
    hidden = values * logistic
    return hidden, logistic + hidden * (1.0 - logistic)


def onehot_rows(row_count, index_row):
    rows = lax.broadcasted_iota(jnp.int16, (row_count, index_row.shape[1]), 0)
    return jnp.where(rows == index_row.astype(jnp.int16), jnp.ones((), BF), jnp.zeros((), BF))


def in_vmem(array):
    return pltpu.with_memory_space_constraint(array, pltpu.VMEM)


def vmem():
    return pl.BlockSpec(memory_space=pltpu.VMEM)


def whole(shape):
    return pl.BlockSpec(shape, lambda *_: (0,) * len(shape))


def serve_kernel(place_ref, *refs):
    members, lists, rows_ref = refs[:GROUP], refs[GROUP:-1], refs[-1]
    entries = [ref.at[i] for ref in lists for i in range(ref.shape[0])]
    groups, cap = len(entries), entries[0].shape[1]
    group, member = place_ref[1], place_ref[2] % GROUP
    for k, nodes_ref in enumerate(members):
        owner = member ^ k
        wanted = jnp.concatenate(
            [entry[pl.ds(group * GROUP + owner, 1), :] for entry in entries], axis=1
        )
        picks = onehot_rows(nodes_ref.shape[0], wanted)
        rows = dot(picks, nodes_ref[...], 0, 0).astype(BF)
        place = pl.ds(pl.multiple_of(owner * cap, cap), cap)
        for j in range(groups):
            rows_ref[group ^ j, place, :] = rows[j * cap : (j + 1) * cap]


def serve(place, lists, members):
    groups, cap = sum(part.shape[0] for part in lists), lists[0].shape[2]
    return pl.pallas_call(
        serve_kernel,
        out_shape=pltpu.VMEM((groups, GROUP * cap, members[0].shape[1]), BF),
        in_specs=[pl.BlockSpec(memory_space=pltpu.SMEM)] + [vmem()] * (GROUP + len(lists)),
        out_specs=vmem(),
        compiler_params=pltpu.CompilerParams(vmem_limit_bytes=VMEM_LIMIT),
        name="serve_rows",
    )(place, members[0], *map(in_vmem, members[1:]), lists[0], *map(in_vmem, lists[1:]))


def prepare_kernel(
    edge_ref, cot_ref, recv_ref, node_ref, w_in_ref, part_ref, cot_t_ref, node_part, w_edge_t
):
    latent = edge_ref.shape[1]

    @pl.when(pl.program_id(0) == 0)
    def _():
        node_part[...] = dot(w_in_ref[2 * latent :, :], node_ref[...], 0, 1).astype(BF)
        w_edge_t[...] = w_in_ref[:latent, :].T

    recv_hot = onehot_rows(node_ref.shape[0], recv_ref[0])
    part_ref[0] = dot(w_edge_t[...], edge_ref[...], 1, 1) + dot(node_part[...], recv_hot, 1, 0)
    cot_t_ref[0] = cot_ref[...].T


def prepare(edge_lat, edge_cot, recv_rows, node_lat, w_edge_in):
    edges, latent = edge_lat.shape
    hidden = w_edge_in.shape[1]
    nodes = node_lat.shape[0]
    chunks = edges // CHUNK
    rows = pl.BlockSpec((CHUNK, latent), lambda i: (i, 0))

    def along(height):
        return pl.BlockSpec((1, height, CHUNK), lambda i: (i, 0, 0))

    return pl.pallas_call(
        prepare_kernel,
        grid=(chunks,),
        out_shape=[
            jax.ShapeDtypeStruct((chunks, hidden, CHUNK), F32),
            jax.ShapeDtypeStruct((chunks, latent, CHUNK), BF),
        ],
        in_specs=[rows, rows, along(1), whole(node_lat.shape), whole(w_edge_in.shape)],
        out_specs=[along(hidden), along(latent)],
        scratch_shapes=[pltpu.VMEM((hidden, nodes), BF), pltpu.VMEM((hidden, latent), BF)],
        compiler_params=pltpu.CompilerParams(vmem_limit_bytes=VMEM_LIMIT),
        cost_estimate=pl.CostEstimate(
            flops=4 * edges * latent * hidden, bytes_accessed=8 * edges * latent, transcendentals=0
        ),
        name="prepare_edges",
    )(edge_lat, edge_cot, recv_rows, node_lat, w_edge_in)


def layer_kernel(
    piece_rows,
    core_ref,
    part_hbm,
    cot_hbm,
    edge_hbm,
    recv_ref,
    slot_ref,
    fetched_ref,
    wanted_ref,
    valid_ref,
    node_ref,
    node_cot_ref,
    w_in_ref,
    w_out_ref,
    gain_edge_ref,
    w_node_in_ref,
    w_node_out_ref,
    gain_node_ref,
    grad_pre_hbm,
    node_local_ref,
    keep_ref,
    send_ref,
    part,
    cot,
    edge,
    hot,
    hidden,
    slope,
    normed,
    scale,
    grad_pre,
    send_part,
    summed_acc,
    w_in_acc,
    w_out_acc,
    ends_acc,
    gain_acc,
    grad_summed,
    weight_pack,
    w_out_t,
    gain_column,
    pack,
    sems,
    out_sems,
):
    chunks, latent, width = part.shape
    nodes = node_ref.shape[0]
    slots = fetched_ref.shape[0]
    bands = pack.shape[1] * 2
    cap = slots // bands

    def part_copy(c):
        return pltpu.make_async_copy(part_hbm.at[c], part.at[c], sems.at[0, c])

    def cot_copy(c):
        return pltpu.make_async_copy(cot_hbm.at[c], cot.at[c], sems.at[1, c])

    def edge_copy(c):
        return pltpu.make_async_copy(edge_hbm.at[c], edge.at[c], sems.at[2, c])

    for copy in (part_copy, cot_copy, edge_copy):
        for c in range(chunks):
            copy(c).start()

    w_out_t[...] = w_out_ref[...].T
    gain_column[...] = jnp.broadcast_to(gain_edge_ref[...], (128, latent)).T
    summed_acc[...] = jnp.zeros_like(summed_acc)
    send_part[...] = dot(w_in_ref[latent : 2 * latent, :], fetched_ref[...], 0, 1).astype(BF)
    for c in range(chunks):
        part_copy(c).wait()
    w_in_acc[...] = jnp.zeros_like(w_in_acc)
    w_out_acc[...] = jnp.zeros_like(w_out_acc)
    ends_acc[...] = jnp.zeros_like(ends_acc)
    gain_acc[...] = jnp.zeros_like(gain_acc)

    @pl.loop(0, chunks, unroll=True)
    def _(c):
        slot_hot = onehot_rows(slots, slot_ref[c])
        recv_hot = onehot_rows(nodes, recv_ref[c])
        hot[c, :nodes, :] = recv_hot
        hot[c, nodes:, :] = slot_hot
        pre = part[c] + dot(send_part[...], slot_hot, 1, 0)
        hid, slo = swish_and_slope(pre)
        hid = hid.astype(BF)
        hidden[c] = hid
        slope[c] = slo.astype(BF)
        out = dot(w_out_t[...], hid, 1, 0)
        centred = out - jnp.mean(out, axis=0, keepdims=True)
        inv = lax.rsqrt(jnp.mean(centred * centred, axis=0, keepdims=True) + epsilon)
        inv = inv * valid_ref[c]
        scale[c] = inv
        norm = (centred * inv).astype(BF)
        normed[c] = norm
        summed_acc[...] += dot(norm, recv_hot, 1, 1)

    for c in range(chunks):
        cot_copy(c).wait()
        edge_copy(c).wait()
    node = node_ref[...]
    summed = (summed_acc[...] * gain_column[:, :1]).astype(BF)
    pre_node = dot(w_node_in_ref[:latent, :], node, 0, 1) + dot(
        w_node_in_ref[latent:, :], summed, 0, 0
    )
    hid_node, slope_node = swish_and_slope(pre_node)
    hid_node = hid_node.astype(BF)
    out_node = dot(w_node_out_ref[...], hid_node, 0, 0)
    centred = out_node - jnp.mean(out_node, axis=0, keepdims=True)
    inv_node = lax.rsqrt(jnp.mean(centred * centred, axis=0, keepdims=True) + epsilon)
    norm_node = centred * inv_node
    node_base = node_cot_ref[...].astype(F32)
    cot_node = node_base.T
    product = cot_node * norm_node
    gain_node_grad = jnp.sum(product.T, axis=0, keepdims=True)
    dy = cot_node * jnp.broadcast_to(gain_node_ref[...], (128, latent)).T[:, :1]
    grad_out_node = (
        inv_node
        * (
            dy
            - jnp.mean(dy, axis=0, keepdims=True)
            - norm_node * jnp.mean(dy * norm_node, axis=0, keepdims=True)
        )
    ).astype(BF)
    base = 4 * latent
    weight_pack[base + 2 * latent : base + 3 * latent, :] = dot(hid_node, grad_out_node, 1, 1)
    grad_pre_node = (dot(w_node_out_ref[...], grad_out_node, 1, 0) * slope_node).astype(BF)
    weight_pack[base : base + latent, :] = dot(node, grad_pre_node, 0, 1)
    weight_pack[base + latent : base + 2 * latent, :] = dot(summed, grad_pre_node, 1, 1)
    grad_summed[...] = dot(w_node_in_ref[latent:, :], grad_pre_node, 1, 0).astype(BF)
    node_local = node_base + dot(grad_pre_node, w_node_in_ref[:latent, :], 0, 1)

    @pl.loop(0, chunks, unroll=True)
    def _(c):
        grad_update = cot[c].astype(F32) + dot(grad_summed[...], hot[c, :nodes, :], 1, 0)
        norm = normed[c].astype(F32)
        product = grad_update * norm
        gain_acc[...] += product
        gain = gain_column[:, :1]
        dy = grad_update * gain
        mean_dy = jnp.mean(dy, axis=0, keepdims=True)
        mean_product = jnp.mean(product * gain, axis=0, keepdims=True)
        grad_out = (scale[c] * (dy - mean_dy - norm * mean_product)).astype(BF)
        w_out_acc[...] += dot(hidden[c], grad_out, 1, 1)
        grad_hidden = dot(w_out_ref[...], grad_out, 1, 0)
        grad_in = (grad_hidden * slope[c].astype(F32)).astype(BF)
        grad_pre[c] = grad_in
        w_in_acc[...] += dot(grad_in, edge[c], 1, 0)
        ends_acc[...] += dot(hot[c], grad_in, 1, 1)

    for c in range(chunks):
        pltpu.make_async_copy(grad_pre.at[c], grad_pre_hbm.at[c], out_sems.at[c]).start()
    recv_sum = ends_acc[:nodes, :].astype(BF)
    slot_sum = ends_acc[nodes:, :].astype(BF)
    node_local_ref[...] = node_local + dot(recv_sum, w_in_ref[2 * latent :, :], 1, 1)
    weight_pack[:latent, :] = w_in_acc[...].T
    weight_pack[latent : 2 * latent, :] = dot(fetched_ref[...], slot_sum, 0, 0)
    weight_pack[2 * latent : 3 * latent, :] = dot(node, recv_sum, 0, 0)
    weight_pack[3 * latent : 4 * latent, :] = w_out_acc[...]
    used = base + 3 * latent
    if used < weight_pack.shape[0]:
        weight_pack[used:, :] = jnp.zeros_like(weight_pack[used:, :])
    gain_edge_grad = jnp.sum(gain_acc[...].T, axis=0, keepdims=True)
    slot_grads = dot(slot_sum, w_in_ref[latent : 2 * latent, :], 1, 1).astype(BF)
    core = core_ref[0]
    for d in range(bands):
        pack[d % 2, d // 2, :cap, :] = slot_grads[d * cap : (d + 1) * cap, :]
        body = weight_pack[d * piece_rows : (d + 1) * piece_rows, :]
        pack[d % 2, d // 2, cap : cap + piece_rows, :] = body.astype(BF)
        row = lax.broadcasted_iota(jnp.int32, (TAIL, latent), 0)
        listed = jnp.concatenate([wanted_ref[d : d + 1, :].astype(F32)] * (latent // cap), axis=1)
        column = lax.broadcasted_iota(jnp.int32, (1, latent), 1)
        listed = jnp.where(column // cap == core, listed, 0.0)
        extra = jnp.where(row == 1, listed, 0.0)
        if d < 2:
            extra = jnp.where(row == 0, gain_edge_grad if d == 0 else gain_node_grad, extra)
        pack[d % 2, d // 2, cap + piece_rows :, :] = extra.astype(BF)
    for own in range(2):

        @pl.when(core == own)
        def _():
            keep_ref[...] = pack[own]
            send_ref[...] = pack[1 - own]

    for c in range(chunks):
        pltpu.make_async_copy(grad_pre.at[c], grad_pre_hbm.at[c], out_sems.at[c]).wait()


def layer(
    core, part, cot_t, edge_lat, recv_rows, slot_rows, fetched, wanted, valid_rows, node_lat, node_cot, weights, bands
):
    chunks, hidden, width = part.shape
    edges = edge_lat.reshape(chunks, width, -1)
    nodes, latent = node_lat.shape
    slots = fetched.shape[0]
    cap = slots // bands
    piece_rows = -(-7 * latent // (bands * 16)) * 16
    hbm = pl.BlockSpec(memory_space=pl.ANY)
    return pl.pallas_call(
        functools.partial(layer_kernel, piece_rows),
        out_shape=[
            jax.ShapeDtypeStruct((chunks, hidden, width), BF),
            jax.ShapeDtypeStruct((nodes, latent), F32),
            pltpu.VMEM((bands // 2, cap + piece_rows + TAIL, latent), BF),
            pltpu.VMEM((bands // 2, cap + piece_rows + TAIL, latent), BF),
        ],
        in_specs=[pl.BlockSpec(memory_space=pltpu.SMEM)] + [hbm] * 3 + [vmem()] * 13,
        out_specs=[hbm, vmem(), vmem(), vmem()],
        scratch_shapes=[
            pltpu.VMEM((chunks, hidden, width), F32),
            pltpu.VMEM((chunks, latent, width), BF),
            pltpu.VMEM((chunks, width, latent), BF),
            pltpu.VMEM((chunks, nodes + slots, width), BF),
            pltpu.VMEM((chunks, hidden, width), BF),
            pltpu.VMEM((chunks, hidden, width), BF),
            pltpu.VMEM((chunks, latent, width), BF),
            pltpu.VMEM((chunks, 1, width), F32),
            pltpu.VMEM((chunks, hidden, width), BF),
            pltpu.VMEM((hidden, slots), BF),
            pltpu.VMEM((latent, nodes), F32),
            pltpu.VMEM((hidden, latent), F32),
            pltpu.VMEM((hidden, latent), F32),
            pltpu.VMEM((nodes + slots, hidden), F32),
            pltpu.VMEM((latent, width), F32),
            pltpu.VMEM((latent, nodes), BF),
            pltpu.VMEM((piece_rows * bands, latent), F32),
            pltpu.VMEM((latent, hidden), BF),
            pltpu.VMEM((latent, 128), F32),
            pltpu.VMEM((2, bands // 2, cap + piece_rows + TAIL, latent), BF),
            pltpu.SemaphoreType.DMA((3, chunks)),
            pltpu.SemaphoreType.DMA((chunks,)),
        ],
        compiler_params=pltpu.CompilerParams(vmem_limit_bytes=VMEM_LIMIT),
        name="layer_backward",
    )(core, part, cot_t, edges, recv_rows, slot_rows, in_vmem(fetched), wanted, valid_rows, node_lat, node_cot, *weights)


def edge_kernel(grad_ref, cot_ref, w_in_ref, out_ref):
    latent = cot_ref.shape[1]
    back = dot(grad_ref[0], w_in_ref[:latent, :], 0, 1)
    out_ref[...] = (cot_ref[...].astype(F32) + back).astype(BF)


def edge_result(grad_pre, edge_cot, w_edge_in):
    chunks, hidden, width = grad_pre.shape
    latent = edge_cot.shape[1]
    rows = pl.BlockSpec((width, latent), lambda i: (i, 0))
    return pl.pallas_call(
        edge_kernel,
        grid=(chunks,),
        out_shape=jax.ShapeDtypeStruct(edge_cot.shape, BF),
        in_specs=[
            pl.BlockSpec((1, hidden, width), lambda i: (i, 0, 0)),
            rows,
            whole(w_edge_in.shape),
        ],
        out_specs=rows,
        compiler_params=pltpu.CompilerParams(vmem_limit_bytes=VMEM_LIMIT),
        cost_estimate=pl.CostEstimate(
            flops=2 * chunks * width * hidden * latent,
            bytes_accessed=6 * chunks * width * latent,
            transcendentals=0,
        ),
        name="edge_result",
    )(grad_pre, edge_cot, w_edge_in)


def join_kernel(cap, keep_ref, got_ref, out_ref):
    out_ref[:, :cap, :] = keep_ref[:, :cap, :]
    out_ref[:, cap : 2 * cap, :] = got_ref[:, :cap, :]
    out_ref[:, 2 * cap :, :] = (
        keep_ref[:, cap:, :].astype(F32) + got_ref[:, cap:, :].astype(F32)
    ).astype(BF)


def join(keep, got, cap):
    chips, height, latent = keep.shape
    return pl.pallas_call(
        functools.partial(join_kernel, cap),
        out_shape=pltpu.VMEM((chips, height + cap, latent), BF),
        in_specs=[vmem(), vmem()],
        out_specs=vmem(),
        name="join_cores",
    )(in_vmem(keep), in_vmem(got))


def total_kernel(sums_ref, pieces_ref):
    chips, height, _ = pieces_ref.shape
    first = sums_ref.shape[1] - height
    piece = jnp.sum(sums_ref[:, first:, :].astype(F32), axis=0).astype(BF)
    for chip in range(chips):
        pieces_ref[chip] = piece


def total(sums, cap):
    chips, height, latent = sums.shape
    return pl.pallas_call(
        total_kernel,
        out_shape=pltpu.VMEM((chips, height - 2 * cap, latent), BF),
        in_specs=[vmem()],
        out_specs=vmem(),
        name="total_piece",
    )(in_vmem(sums))


def settle_kernel(cap, core_ref, back_ref, local_ref, node_grad_ref):
    chips, height, latent = back_ref.shape
    rows = back_ref[:, : 2 * cap, :].reshape(chips * 2 * cap, latent)
    core = core_ref[0]
    listed = back_ref[:, height - TAIL + 1, :].astype(F32)
    lists = []
    for chip in range(chips):
        first, second = listed[chip : chip + 1, :cap], listed[chip : chip + 1, cap : 2 * cap]
        lists.append(jnp.where(core == 0, first, second))
        lists.append(jnp.where(core == 0, second, first))
    picks = onehot_rows(local_ref.shape[0], jnp.concatenate(lists, axis=1).astype(jnp.int32))
    node_grad_ref[...] = local_ref[...] + dot(picks, rows, 1, 0)


def settle(place, back, node_local, cap):
    return pl.pallas_call(
        functools.partial(settle_kernel, cap),
        out_shape=jax.ShapeDtypeStruct(node_local.shape, F32),
        in_specs=[pl.BlockSpec(memory_space=pltpu.SMEM)] + [vmem()] * 2,
        out_specs=vmem(),
        name="settle_sums",
    )(place, in_vmem(back), node_local)


def assemble_kernel(core_ref, mine_ref, theirs_ref, *refs):
    outs, (rows, out_sems) = refs[:-2], refs[-2:]
    chips, height, latent = mine_ref.shape
    body = height - TAIL
    core = core_ref[0]
    starts, at = [], 0
    for out in outs[:-2]:
        starts.append(at)
        at += out.shape[0]

    def outgoing(k):
        source = rows.at[pl.ds(starts[k], outs[k].shape[0])]
        return pltpu.make_async_copy(source, outs[k], out_sems.at[k])

    sent = 0
    for chip in range(chips):
        for side, ref in enumerate((mine_ref, theirs_ref)):
            place = 2 * chip + (core if side == 0 else 1 - core)
            rows[pl.ds(pl.multiple_of(place * body, body), body), :] = ref[
                chip, :body, :
            ].astype(F32)
        if chip == 0:
            first, second = mine_ref[0, body:, :].astype(F32), theirs_ref[0, body:, :].astype(F32)
            outs[-2][...] = jnp.where(core == 0, first, second)[:1]
            outs[-1][...] = jnp.where(core == 0, second, first)[:1]
        while sent < len(starts) and starts[sent] + outs[sent].shape[0] <= 2 * (chip + 1) * body:
            outgoing(sent).start()
            sent += 1
    for k in range(len(starts)):
        outgoing(k).wait()


def assemble(place, mine, theirs, latent):
    chips, height, width = mine.shape
    heights = (3 * latent, latent, 2 * latent, latent, 1, 1)
    hbm = pl.BlockSpec(memory_space=pl.ANY)
    return pl.pallas_call(
        assemble_kernel,
        out_shape=[jax.ShapeDtypeStruct((rows, width), F32) for rows in heights],
        in_specs=[pl.BlockSpec(memory_space=pltpu.SMEM), vmem(), vmem()],
        out_specs=[hbm] * 4 + [vmem()] * 2,
        scratch_shapes=[
            pltpu.VMEM((2 * chips * (height - TAIL), width), F32),
            pltpu.SemaphoreType.DMA((4,)),
        ],
        compiler_params=pltpu.CompilerParams(vmem_limit_bytes=VMEM_LIMIT),
        name="assemble_sums",
    )(place, in_vmem(mine), in_vmem(theirs))


def per_device(
    node_lat,
    edge_lat,
    node_cot,
    edge_cot,
    w_edge_in,
    w_edge_out,
    gain_edge,
    w_node_in,
    w_node_out,
    gain_node,
    fetch_idx,
    edge_slot,
    edge_recv,
    block_fill,
):
    bands = lax.axis_size("band")
    chips = bands // 2
    me = lax.axis_index("band")
    place = jnp.stack([me % 2, me // GROUP, me]).astype(jnp.int32)
    latent = node_lat.shape[1]
    cap = fetch_idx.shape[2]
    slots = bands * cap
    chunks = edge_lat.shape[0] // CHUNK
    other_core = [(i, i ^ 1) for i in range(bands)]
    same_core = [[2 * i + c for i in range(chips)] for c in range(2)]

    groups = bands // GROUP
    like_placed = [[GROUP * g + i for g in range(groups)] for i in range(GROUP)]

    def swap(array, step):
        return lax.ppermute(array, "band", [(i, i ^ step) for i in range(bands)])

    across = swap(node_lat, 2)
    lists = [fetch_idx]
    step = GROUP
    while step < bands:
        held = lists[0] if len(lists) == 1 else jnp.concatenate(lists, axis=0)
        lists.append(swap(held, step))
        step *= 2
    members = (node_lat, swap(node_lat, 1), across, swap(across, 1))
    rows = serve(place, lists, members)
    valid = jnp.arange(128, dtype=jnp.int32)[None, :] < block_fill[0][:, None]
    valid = valid.astype(F32).reshape(chunks, 1, CHUNK)
    recv_rows = edge_recv.reshape(chunks, 1, CHUNK)
    w_edge_first, rows = lax.optimization_barrier((w_edge_in, rows))
    fetched = lax.all_to_all(
        rows, "band", split_axis=0, concat_axis=0, tiled=True, axis_index_groups=like_placed
    ).reshape(slots, latent)

    slot_rows = edge_slot.reshape(chunks, 1, CHUNK)
    part, cot_t = prepare(
        edge_lat, edge_cot, recv_rows, node_lat, w_edge_first
    )
    weights = (
        w_edge_in,
        w_edge_out,
        gain_edge[None, :],
        w_node_in,
        w_node_out,
        gain_node[None, :],
    )
    grad_pre, node_local, keep, send = layer(
        place,
        part,
        cot_t,
        edge_lat,
        recv_rows,
        slot_rows,
        fetched,
        fetch_idx[0],
        valid,
        node_lat,
        node_cot,
        weights,
        bands,
    )
    got = lax.ppermute(send, "band", other_core)
    joined = join(keep, got, cap)
    back = lax.all_to_all(
        joined, "band", split_axis=0, concat_axis=0, tiled=True, axis_index_groups=same_core
    )
    edge_grad = edge_result(grad_pre, edge_cot, w_edge_in)
    back, edge_grad = lax.optimization_barrier((back, edge_grad))
    pieces = total(back, cap)
    mine = lax.all_to_all(
        pieces, "band", split_axis=0, concat_axis=0, tiled=True, axis_index_groups=same_core
    )
    node_grad = settle(place, back, node_local, cap)
    mine, node_grad = lax.optimization_barrier((mine, node_grad))
    theirs = lax.ppermute(mine, "band", other_core)
    sums = assemble(place, mine, theirs, latent)
    return (
        node_grad,
        edge_grad,
        sums[0],
        sums[1],
        sums[4].reshape(-1),
        sums[2],
        sums[3],
        sums[5].reshape(-1),
    )


def solution(mesh):
    in_specs = (
        P(("grp", "band"), None),
        P(("grp", "band"), None),
        P(("grp", "band"), None),
        P(("grp", "band"), None),
        P(),
        P(),
        P(),
        P(),
        P(),
        P(),
        P("band", None, None),
        P("band"),
        P("band"),
        P("band", None),
    )
    out_specs = (
        P(("grp", "band"), None),
        P(("grp", "band"), None),
        P("grp", None),
        P("grp", None),
        P("grp"),
        P("grp", None),
        P("grp", None),
        P("grp"),
    )
    return jax.shard_map(
        per_device, mesh=mesh, in_specs=in_specs, out_specs=out_specs, check_vma=False
    )
```

```python
import functools

import jax
import jax.numpy as jnp
from jax import lax
from jax.experimental import pallas as pl
from jax.experimental.pallas import tpu as pltpu
from jax.sharding import PartitionSpec as P

epsilon = 1e-05
CHUNK = 1280
GROUP = 4
TAIL = 8
VMEM_LIMIT = 60 * 2**20
BF = jnp.bfloat16
F32 = jnp.float32


def dot(lhs, rhs, lhs_dim, rhs_dim):
    return lax.dot_general(
        lhs, rhs, (((lhs_dim,), (rhs_dim,)), ((), ())), preferred_element_type=F32
    )


def swish_and_slope(values):
    logistic = jax.nn.sigmoid(values)
    hidden = values * logistic
    return hidden, logistic + hidden * (1.0 - logistic)


def onehot_rows(row_count, index_row):
    rows = lax.broadcasted_iota(jnp.int16, (row_count, index_row.shape[1]), 0)
    return jnp.where(rows == index_row.astype(jnp.int16), jnp.ones((), BF), jnp.zeros((), BF))


def in_vmem(array):
    return pltpu.with_memory_space_constraint(array, pltpu.VMEM)


def vmem():
    return pl.BlockSpec(memory_space=pltpu.VMEM)


def whole(shape):
    return pl.BlockSpec(shape, lambda *_: (0,) * len(shape))


def serve_kernel(place_ref, *refs):
    members, lists, rows_ref = refs[:GROUP], refs[GROUP:-1], refs[-1]
    entries = [ref.at[i] for ref in lists for i in range(ref.shape[0])]
    groups, cap = len(entries), entries[0].shape[1]
    group, member = place_ref[1], place_ref[2] % GROUP
    for k, nodes_ref in enumerate(members):
        owner = member ^ k
        wanted = jnp.concatenate(
            [entry[pl.ds(group * GROUP + owner, 1), :] for entry in entries], axis=1
        )
        picks = onehot_rows(nodes_ref.shape[0], wanted)
        rows = dot(picks, nodes_ref[...], 0, 0).astype(BF)
        place = pl.ds(pl.multiple_of(owner * cap, cap), cap)
        for j in range(groups):
            rows_ref[group ^ j, place, :] = rows[j * cap : (j + 1) * cap]


def serve(place, lists, members):
    groups, cap = sum(part.shape[0] for part in lists), lists[0].shape[2]
    return pl.pallas_call(
        serve_kernel,
        out_shape=pltpu.VMEM((groups, GROUP * cap, members[0].shape[1]), BF),
        in_specs=[pl.BlockSpec(memory_space=pltpu.SMEM)] + [vmem()] * (GROUP + len(lists)),
        out_specs=vmem(),
        compiler_params=pltpu.CompilerParams(vmem_limit_bytes=VMEM_LIMIT),
        name="serve_rows",
    )(place, members[0], *map(in_vmem, members[1:]), lists[0], *map(in_vmem, lists[1:]))


def prepare_kernel(
    edge_ref, cot_ref, recv_ref, node_ref, w_in_ref, part_ref, cot_t_ref, node_part, w_edge_t
):
    latent = edge_ref.shape[1]

    @pl.when(pl.program_id(0) == 0)
    def _():
        node_part[...] = dot(w_in_ref[2 * latent :, :], node_ref[...], 0, 1).astype(BF)
        w_edge_t[...] = w_in_ref[:latent, :].T

    recv_hot = onehot_rows(node_ref.shape[0], recv_ref[0])
    part_ref[0] = dot(w_edge_t[...], edge_ref[...], 1, 1) + dot(node_part[...], recv_hot, 1, 0)
    cot_t_ref[0] = cot_ref[...].T


def prepare(edge_lat, edge_cot, recv_rows, node_lat, w_edge_in):
    edges, latent = edge_lat.shape
    hidden = w_edge_in.shape[1]
    nodes = node_lat.shape[0]
    chunks = edges // CHUNK
    rows = pl.BlockSpec((CHUNK, latent), lambda i: (i, 0))

    def along(height):
        return pl.BlockSpec((1, height, CHUNK), lambda i: (i, 0, 0))

    return pl.pallas_call(
        prepare_kernel,
        grid=(chunks,),
        out_shape=[
            jax.ShapeDtypeStruct((chunks, hidden, CHUNK), F32),
            jax.ShapeDtypeStruct((chunks, latent, CHUNK), BF),
        ],
        in_specs=[rows, rows, along(1), whole(node_lat.shape), whole(w_edge_in.shape)],
        out_specs=[along(hidden), along(latent)],
        scratch_shapes=[pltpu.VMEM((hidden, nodes), BF), pltpu.VMEM((hidden, latent), BF)],
        compiler_params=pltpu.CompilerParams(vmem_limit_bytes=VMEM_LIMIT),
        cost_estimate=pl.CostEstimate(
            flops=4 * edges * latent * hidden, bytes_accessed=8 * edges * latent, transcendentals=0
        ),
        name="prepare_edges",
    )(edge_lat, edge_cot, recv_rows, node_lat, w_edge_in)


def layer_kernel(
    piece_rows,
    core_ref,
    part_hbm,
    cot_hbm,
    edge_hbm,
    recv_ref,
    slot_ref,
    fetched_ref,
    wanted_ref,
    valid_ref,
    node_ref,
    node_cot_ref,
    w_in_ref,
    w_out_ref,
    gain_edge_ref,
    w_node_in_ref,
    w_node_out_ref,
    gain_node_ref,
    grad_pre_hbm,
    node_local_ref,
    keep_ref,
    send_ref,
    part,
    cot,
    edge,
    hot,
    hidden,
    slope,
    normed,
    scale,
    grad_pre,
    send_part,
    summed_acc,
    w_in_acc,
    w_out_acc,
    ends_acc,
    gain_acc,
    grad_summed,
    weight_pack,
    w_out_t,
    gain_column,
    sems,
    out_sems,
):
    chunks, latent, width = part.shape
    nodes = node_ref.shape[0]
    slots = fetched_ref.shape[0]
    bands = keep_ref.shape[0] * 2
    cap = slots // bands

    def part_copy(c):
        return pltpu.make_async_copy(part_hbm.at[c], part.at[c], sems.at[0, c])

    def cot_copy(c):
        return pltpu.make_async_copy(cot_hbm.at[c], cot.at[c], sems.at[1, c])

    def edge_copy(c):
        return pltpu.make_async_copy(edge_hbm.at[c], edge.at[c], sems.at[2, c])

    for copy in (part_copy, cot_copy, edge_copy):
        for c in range(chunks):
            copy(c).start()

    w_out_t[...] = w_out_ref[...].T
    gain_column[...] = jnp.broadcast_to(gain_edge_ref[...], (128, latent)).T
    summed_acc[...] = jnp.zeros_like(summed_acc)
    send_part[...] = dot(w_in_ref[latent : 2 * latent, :], fetched_ref[...], 0, 1).astype(BF)
    w_in_acc[...] = jnp.zeros_like(w_in_acc)
    w_out_acc[...] = jnp.zeros_like(w_out_acc)
    ends_acc[...] = jnp.zeros_like(ends_acc)
    gain_acc[...] = jnp.zeros_like(gain_acc)

    for c in range(chunks):
        for arrived in range(1) if c == 0 else range(1, chunks) if c == 1 else ():
            part_copy(arrived).wait()
        slot_hot = onehot_rows(slots, slot_ref[c])
        recv_hot = onehot_rows(nodes, recv_ref[c])
        hot[c, :nodes, :] = recv_hot
        hot[c, nodes:, :] = slot_hot
        pre = part[c] + dot(send_part[...], slot_hot, 1, 0)
        hid, slo = swish_and_slope(pre)
        hid = hid.astype(BF)
        hidden[c] = hid
        slope[c] = slo.astype(BF)
        out = dot(w_out_t[...], hid, 1, 0)
        centred = out - jnp.mean(out, axis=0, keepdims=True)
        inv = lax.rsqrt(jnp.mean(centred * centred, axis=0, keepdims=True) + epsilon)
        inv = inv * valid_ref[c]
        scale[c] = inv
        norm = (centred * inv).astype(BF)
        normed[c] = norm
        summed_acc[...] += dot(norm, recv_hot, 1, 1)

    for c in range(chunks):
        cot_copy(c).wait()
        edge_copy(c).wait()
    node = node_ref[...]
    summed = (summed_acc[...] * gain_column[:, :1]).astype(BF)
    pre_node = dot(w_node_in_ref[:latent, :], node, 0, 1) + dot(
        w_node_in_ref[latent:, :], summed, 0, 0
    )
    hid_node, slope_node = swish_and_slope(pre_node)
    hid_node = hid_node.astype(BF)
    out_node = dot(w_node_out_ref[...], hid_node, 0, 0)
    centred = out_node - jnp.mean(out_node, axis=0, keepdims=True)
    inv_node = lax.rsqrt(jnp.mean(centred * centred, axis=0, keepdims=True) + epsilon)
    norm_node = centred * inv_node
    node_base = node_cot_ref[...].astype(F32)
    cot_node = node_base.T
    product = cot_node * norm_node
    gain_node_grad = jnp.sum(product.T, axis=0, keepdims=True)
    dy = cot_node * jnp.broadcast_to(gain_node_ref[...], (128, latent)).T[:, :1]
    grad_out_node = (
        inv_node
        * (
            dy
            - jnp.mean(dy, axis=0, keepdims=True)
            - norm_node * jnp.mean(dy * norm_node, axis=0, keepdims=True)
        )
    ).astype(BF)
    base = 4 * latent
    weight_pack[base + 2 * latent : base + 3 * latent, :] = dot(hid_node, grad_out_node, 1, 1)
    grad_pre_node = (dot(w_node_out_ref[...], grad_out_node, 1, 0) * slope_node).astype(BF)
    weight_pack[base : base + latent, :] = dot(node, grad_pre_node, 0, 1)
    weight_pack[base + latent : base + 2 * latent, :] = dot(summed, grad_pre_node, 1, 1)
    grad_summed[...] = dot(w_node_in_ref[latent:, :], grad_pre_node, 1, 0).astype(BF)
    node_local = node_base + dot(grad_pre_node, w_node_in_ref[:latent, :], 0, 1)

    @pl.loop(0, chunks, unroll=True)
    def _(c):
        grad_update = cot[c].astype(F32) + dot(grad_summed[...], hot[c, :nodes, :], 1, 0)
        norm = normed[c].astype(F32)
        product = grad_update * norm
        gain_acc[...] += product
        gain = gain_column[:, :1]
        dy = grad_update * gain
        mean_dy = jnp.mean(dy, axis=0, keepdims=True)
        mean_product = jnp.mean(product * gain, axis=0, keepdims=True)
        grad_out = (scale[c] * (dy - mean_dy - norm * mean_product)).astype(BF)
        w_out_acc[...] += dot(hidden[c], grad_out, 1, 1)
        grad_hidden = dot(w_out_ref[...], grad_out, 1, 0)
        grad_in = (grad_hidden * slope[c].astype(F32)).astype(BF)
        grad_pre[c] = grad_in
        w_in_acc[...] += dot(grad_in, edge[c], 1, 0)
        ends_acc[...] += dot(hot[c], grad_in, 1, 1)

    for c in range(chunks):
        pltpu.make_async_copy(grad_pre.at[c], grad_pre_hbm.at[c], out_sems.at[c]).start()
    recv_sum = ends_acc[:nodes, :].astype(BF)
    slot_sum = ends_acc[nodes:, :].astype(BF)
    node_local_ref[...] = node_local + dot(recv_sum, w_in_ref[2 * latent :, :], 1, 1)
    weight_pack[:latent, :] = w_in_acc[...].T
    weight_pack[latent : 2 * latent, :] = dot(fetched_ref[...], slot_sum, 0, 0)
    weight_pack[2 * latent : 3 * latent, :] = dot(node, recv_sum, 0, 0)
    weight_pack[3 * latent : 4 * latent, :] = w_out_acc[...]
    used = base + 3 * latent
    if used < weight_pack.shape[0]:
        weight_pack[used:, :] = jnp.zeros_like(weight_pack[used:, :])
    gain_edge_grad = jnp.sum(gain_acc[...].T, axis=0, keepdims=True)
    slot_grads = dot(slot_sum, w_in_ref[latent : 2 * latent, :], 1, 1).astype(BF)
    core = core_ref[0]
    row = lax.broadcasted_iota(jnp.int32, (TAIL, latent), 0)
    column = lax.broadcasted_iota(jnp.int32, (1, latent), 1)
    for own in range(2):

        @pl.when(core == own)
        def _():
            for d in range(bands):
                out = (keep_ref if d % 2 == own else send_ref).at[d // 2]
                out[:cap, :] = slot_grads[d * cap : (d + 1) * cap, :]
                body = weight_pack[d * piece_rows : (d + 1) * piece_rows, :]
                out[cap : cap + piece_rows, :] = body.astype(BF)
                listed = jnp.concatenate(
                    [wanted_ref[d : d + 1, :].astype(F32)] * (latent // cap), axis=1
                )
                extra = jnp.where(row == 1, jnp.where(column // cap == own, listed, 0.0), 0.0)
                if d < 2:
                    extra = jnp.where(row == 0, gain_edge_grad if d == 0 else gain_node_grad, extra)
                out[cap + piece_rows :, :] = extra.astype(BF)

    for c in range(chunks):
        pltpu.make_async_copy(grad_pre.at[c], grad_pre_hbm.at[c], out_sems.at[c]).wait()


def layer(
    core, part, cot_t, edge_lat, recv_rows, slot_rows, fetched, wanted, valid_rows, node_lat, node_cot, weights, bands
):
    chunks, hidden, width = part.shape
    edges = edge_lat.reshape(chunks, width, -1)
    nodes, latent = node_lat.shape
    slots = fetched.shape[0]
    cap = slots // bands
    piece_rows = -(-7 * latent // (bands * 16)) * 16
    hbm = pl.BlockSpec(memory_space=pl.ANY)
    return pl.pallas_call(
        functools.partial(layer_kernel, piece_rows),
        out_shape=[
            jax.ShapeDtypeStruct((chunks, hidden, width), BF),
            jax.ShapeDtypeStruct((nodes, latent), F32),
            pltpu.VMEM((bands // 2, cap + piece_rows + TAIL, latent), BF),
            pltpu.VMEM((bands // 2, cap + piece_rows + TAIL, latent), BF),
        ],
        in_specs=[pl.BlockSpec(memory_space=pltpu.SMEM)] + [hbm] * 3 + [vmem()] * 13,
        out_specs=[hbm, vmem(), vmem(), vmem()],
        scratch_shapes=[
            pltpu.VMEM((chunks, hidden, width), F32),
            pltpu.VMEM((chunks, latent, width), BF),
            pltpu.VMEM((chunks, width, latent), BF),
            pltpu.VMEM((chunks, nodes + slots, width), BF),
            pltpu.VMEM((chunks, hidden, width), BF),
            pltpu.VMEM((chunks, hidden, width), BF),
            pltpu.VMEM((chunks, latent, width), BF),
            pltpu.VMEM((chunks, 1, width), F32),
            pltpu.VMEM((chunks, hidden, width), BF),
            pltpu.VMEM((hidden, slots), BF),
            pltpu.VMEM((latent, nodes), F32),
            pltpu.VMEM((hidden, latent), F32),
            pltpu.VMEM((hidden, latent), F32),
            pltpu.VMEM((nodes + slots, hidden), F32),
            pltpu.VMEM((latent, width), F32),
            pltpu.VMEM((latent, nodes), BF),
            pltpu.VMEM((piece_rows * bands, latent), F32),
            pltpu.VMEM((latent, hidden), BF),
            pltpu.VMEM((latent, 128), F32),
            pltpu.SemaphoreType.DMA((3, chunks)),
            pltpu.SemaphoreType.DMA((chunks,)),
        ],
        compiler_params=pltpu.CompilerParams(vmem_limit_bytes=VMEM_LIMIT),
        name="layer_backward",
    )(core, part, cot_t, edges, recv_rows, slot_rows, in_vmem(fetched), wanted, valid_rows, node_lat, node_cot, *weights)


def edge_kernel(grad_ref, cot_ref, w_in_ref, out_ref):
    latent = cot_ref.shape[1]
    back = dot(grad_ref[0], w_in_ref[:latent, :], 0, 1)
    out_ref[...] = (cot_ref[...].astype(F32) + back).astype(BF)


def edge_result(grad_pre, edge_cot, w_edge_in):
    chunks, hidden, width = grad_pre.shape
    latent = edge_cot.shape[1]
    rows = pl.BlockSpec((width, latent), lambda i: (i, 0))
    return pl.pallas_call(
        edge_kernel,
        grid=(chunks,),
        out_shape=jax.ShapeDtypeStruct(edge_cot.shape, BF),
        in_specs=[
            pl.BlockSpec((1, hidden, width), lambda i: (i, 0, 0)),
            rows,
            whole(w_edge_in.shape),
        ],
        out_specs=rows,
        compiler_params=pltpu.CompilerParams(vmem_limit_bytes=VMEM_LIMIT),
        cost_estimate=pl.CostEstimate(
            flops=2 * chunks * width * hidden * latent,
            bytes_accessed=6 * chunks * width * latent,
            transcendentals=0,
        ),
        name="edge_result",
    )(grad_pre, edge_cot, w_edge_in)


def join_kernel(cap, keep_ref, got_ref, out_ref):
    out_ref[:, :cap, :] = keep_ref[:, :cap, :]
    out_ref[:, cap : 2 * cap, :] = got_ref[:, :cap, :]
    out_ref[:, 2 * cap :, :] = (
        keep_ref[:, cap:, :].astype(F32) + got_ref[:, cap:, :].astype(F32)
    ).astype(BF)


def join(keep, got, cap):
    chips, height, latent = keep.shape
    return pl.pallas_call(
        functools.partial(join_kernel, cap),
        out_shape=pltpu.VMEM((chips, height + cap, latent), BF),
        in_specs=[vmem(), vmem()],
        out_specs=vmem(),
        name="join_cores",
    )(in_vmem(keep), in_vmem(got))


def total_kernel(sums_ref, pieces_ref):
    chips, height, _ = pieces_ref.shape
    first = sums_ref.shape[1] - height
    piece = jnp.sum(sums_ref[:, first:, :].astype(F32), axis=0).astype(BF)
    for chip in range(chips):
        pieces_ref[chip] = piece


def total(sums, cap):
    chips, height, latent = sums.shape
    return pl.pallas_call(
        total_kernel,
        out_shape=pltpu.VMEM((chips, height - 2 * cap, latent), BF),
        in_specs=[vmem()],
        out_specs=vmem(),
        name="total_piece",
    )(in_vmem(sums))


def settle_kernel(cap, core_ref, back_ref, local_ref, node_grad_ref):
    chips, height, latent = back_ref.shape
    rows = back_ref[:, : 2 * cap, :].reshape(chips * 2 * cap, latent)
    core = core_ref[0]
    listed = back_ref[:, height - TAIL + 1, :].astype(F32)
    lists = []
    for chip in range(chips):
        first, second = listed[chip : chip + 1, :cap], listed[chip : chip + 1, cap : 2 * cap]
        lists.append(jnp.where(core == 0, first, second))
        lists.append(jnp.where(core == 0, second, first))
    picks = onehot_rows(local_ref.shape[0], jnp.concatenate(lists, axis=1).astype(jnp.int32))
    node_grad_ref[...] = local_ref[...] + dot(picks, rows, 1, 0)


def settle(place, back, node_local, cap):
    return pl.pallas_call(
        functools.partial(settle_kernel, cap),
        out_shape=jax.ShapeDtypeStruct(node_local.shape, F32),
        in_specs=[pl.BlockSpec(memory_space=pltpu.SMEM)] + [vmem()] * 2,
        out_specs=vmem(),
        name="settle_sums",
    )(place, in_vmem(back), node_local)


def assemble_kernel(core_ref, mine_ref, theirs_ref, *refs):
    outs, (rows, out_sems) = refs[:-2], refs[-2:]
    chips, height, latent = mine_ref.shape
    body = height - TAIL
    core = core_ref[0]
    starts, at = [], 0
    for out in outs[:-2]:
        starts.append(at)
        at += out.shape[0]

    def outgoing(k):
        source = rows.at[pl.ds(starts[k], outs[k].shape[0])]
        return pltpu.make_async_copy(source, outs[k], out_sems.at[k])

    sent = 0
    for chip in range(chips):
        for side, ref in enumerate((mine_ref, theirs_ref)):
            place = 2 * chip + (core if side == 0 else 1 - core)
            rows[pl.ds(pl.multiple_of(place * body, body), body), :] = ref[
                chip, :body, :
            ].astype(F32)
        if chip == 0:
            first, second = mine_ref[0, body:, :].astype(F32), theirs_ref[0, body:, :].astype(F32)
            outs[-2][...] = jnp.where(core == 0, first, second)[:1]
            outs[-1][...] = jnp.where(core == 0, second, first)[:1]
        while sent < len(starts) and starts[sent] + outs[sent].shape[0] <= 2 * (chip + 1) * body:
            outgoing(sent).start()
            sent += 1
    for k in range(len(starts)):
        outgoing(k).wait()


def assemble(place, mine, theirs, latent):
    chips, height, width = mine.shape
    heights = (3 * latent, latent, 2 * latent, latent, 1, 1)
    hbm = pl.BlockSpec(memory_space=pl.ANY)
    return pl.pallas_call(
        assemble_kernel,
        out_shape=[jax.ShapeDtypeStruct((rows, width), F32) for rows in heights],
        in_specs=[pl.BlockSpec(memory_space=pltpu.SMEM), vmem(), vmem()],
        out_specs=[hbm] * 4 + [vmem()] * 2,
        scratch_shapes=[
            pltpu.VMEM((2 * chips * (height - TAIL), width), F32),
            pltpu.SemaphoreType.DMA((4,)),
        ],
        compiler_params=pltpu.CompilerParams(vmem_limit_bytes=VMEM_LIMIT),
        name="assemble_sums",
    )(place, in_vmem(mine), in_vmem(theirs))


def per_device(
    node_lat,
    edge_lat,
    node_cot,
    edge_cot,
    w_edge_in,
    w_edge_out,
    gain_edge,
    w_node_in,
    w_node_out,
    gain_node,
    fetch_idx,
    edge_slot,
    edge_recv,
    block_fill,
):
    bands = lax.axis_size("band")
    chips = bands // 2
    me = lax.axis_index("band")
    place = jnp.stack([me % 2, me // GROUP, me]).astype(jnp.int32)
    latent = node_lat.shape[1]
    cap = fetch_idx.shape[2]
    slots = bands * cap
    chunks = edge_lat.shape[0] // CHUNK
    other_core = [(i, i ^ 1) for i in range(bands)]
    same_core = [[2 * i + c for i in range(chips)] for c in range(2)]

    groups = bands // GROUP
    like_placed = [[GROUP * g + i for g in range(groups)] for i in range(GROUP)]

    def swap(array, step):
        return lax.ppermute(array, "band", [(i, i ^ step) for i in range(bands)])

    lists = [fetch_idx]
    step = GROUP
    while step < bands:
        held = lists[0] if len(lists) == 1 else jnp.concatenate(lists, axis=0)
        lists.append(swap(held, step))
        step *= 2
    across = swap(node_lat, 2)
    members = (node_lat, swap(node_lat, 1), across, swap(across, 1))
    rows = serve(place, lists, members)
    valid = jnp.arange(128, dtype=jnp.int32)[None, :] < block_fill[0][:, None]
    valid = valid.astype(F32).reshape(chunks, 1, CHUNK)
    recv_rows = edge_recv.reshape(chunks, 1, CHUNK)
    w_edge_first, rows = lax.optimization_barrier((w_edge_in, rows))
    fetched = lax.all_to_all(
        rows, "band", split_axis=0, concat_axis=0, tiled=True, axis_index_groups=like_placed
    ).reshape(slots, latent)

    slot_rows = edge_slot.reshape(chunks, 1, CHUNK)
    part, cot_t = prepare(
        edge_lat, edge_cot, recv_rows, node_lat, w_edge_first
    )
    weights = (
        w_edge_in,
        w_edge_out,
        gain_edge[None, :],
        w_node_in,
        w_node_out,
        gain_node[None, :],
    )
    grad_pre, node_local, keep, send = layer(
        place,
        part,
        cot_t,
        edge_lat,
        recv_rows,
        slot_rows,
        fetched,
        fetch_idx[0],
        valid,
        node_lat,
        node_cot,
        weights,
        bands,
    )
    got = lax.ppermute(send, "band", other_core)
    joined = join(keep, got, cap)
    back = lax.all_to_all(
        joined, "band", split_axis=0, concat_axis=0, tiled=True, axis_index_groups=same_core
    )
    edge_grad = edge_result(grad_pre, edge_cot, w_edge_in)
    back, edge_grad = lax.optimization_barrier((back, edge_grad))
    pieces = total(back, cap)
    mine = lax.all_to_all(
        pieces, "band", split_axis=0, concat_axis=0, tiled=True, axis_index_groups=same_core
    )
    node_grad = settle(place, back, node_local, cap)
    mine, node_grad = lax.optimization_barrier((mine, node_grad))
    theirs = lax.ppermute(mine, "band", other_core)
    sums = assemble(place, mine, theirs, latent)
    return (
        node_grad,
        edge_grad,
        sums[0],
        sums[1],
        sums[4].reshape(-1),
        sums[2],
        sums[3],
        sums[5].reshape(-1),
    )


def solution(mesh):
    in_specs = (
        P(("grp", "band"), None),
        P(("grp", "band"), None),
        P(("grp", "band"), None),
        P(("grp", "band"), None),
        P(),
        P(),
        P(),
        P(),
        P(),
        P(),
        P("band", None, None),
        P("band"),
        P("band"),
        P("band", None),
    )
    out_specs = (
        P(("grp", "band"), None),
        P(("grp", "band"), None),
        P("grp", None),
        P("grp", None),
        P("grp"),
        P("grp", None),
        P("grp", None),
        P("grp"),
    )
    return jax.shard_map(
        per_device, mesh=mesh, in_specs=in_specs, out_specs=out_specs, check_vma=False
    )
```

```python
import functools

import jax
import jax.numpy as jnp
from jax import lax
from jax.experimental import pallas as pl
from jax.experimental.pallas import tpu as pltpu
from jax.sharding import PartitionSpec as P

epsilon = 1e-05
CHUNK = 1280
GROUP = 4
TAIL = 8
VMEM_LIMIT = 20 * 2**20
LAYER_VMEM_LIMIT = 48 * 2**20
STORED_SLOTS = 1024
BF = jnp.bfloat16
F32 = jnp.float32


def dot(lhs, rhs, lhs_dim, rhs_dim):
    return lax.dot_general(
        lhs, rhs, (((lhs_dim,), (rhs_dim,)), ((), ())), preferred_element_type=F32
    )


def swish_and_slope(values):
    logistic = jax.nn.sigmoid(values)
    hidden = values * logistic
    return hidden, logistic + hidden * (1.0 - logistic)


def onehot_rows(row_count, index_row):
    rows = lax.broadcasted_iota(jnp.int16, (row_count, index_row.shape[1]), 0)
    return jnp.where(rows == index_row.astype(jnp.int16), jnp.ones((), BF), jnp.zeros((), BF))


def in_vmem(array):
    return pltpu.with_memory_space_constraint(array, pltpu.VMEM)


def in_hbm(array):
    return pltpu.with_memory_space_constraint(array, pltpu.HBM)


def vmem():
    return pl.BlockSpec(memory_space=pltpu.VMEM)


def whole(shape):
    return pl.BlockSpec(shape, lambda *_: (0,) * len(shape))


def serve_kernel(place_ref, *refs):
    members, lists, rows_ref = refs[:GROUP], refs[GROUP:-1], refs[-1]
    entries = [ref.at[i] for ref in lists for i in range(ref.shape[0])]
    groups, cap = len(entries), entries[0].shape[1]
    group, member = place_ref[1], place_ref[2] % GROUP
    for k, nodes_ref in enumerate(members):
        owner = member ^ k
        wanted = jnp.concatenate(
            [entry[pl.ds(group * GROUP + owner, 1), :] for entry in entries], axis=1
        )
        picks = onehot_rows(nodes_ref.shape[0], wanted)
        rows = dot(picks, nodes_ref[...], 0, 0).astype(BF)
        place = pl.ds(pl.multiple_of(owner * cap, cap), cap)
        for j in range(groups):
            rows_ref[group ^ j, place, :] = rows[j * cap : (j + 1) * cap]


def serve(place, lists, members):
    groups, cap = sum(part.shape[0] for part in lists), lists[0].shape[2]
    return pl.pallas_call(
        serve_kernel,
        out_shape=pltpu.VMEM((groups, GROUP * cap, members[0].shape[1]), BF),
        in_specs=[pl.BlockSpec(memory_space=pltpu.SMEM)] + [vmem()] * (GROUP + len(lists)),
        out_specs=vmem(),
        compiler_params=pltpu.CompilerParams(vmem_limit_bytes=VMEM_LIMIT),
        name="serve_rows",
    )(place, in_hbm(members[0]), *map(in_vmem, members[1:]), in_hbm(lists[0]), *map(in_vmem, lists[1:]))


def prepare_kernel(
    edge_ref, cot_ref, recv_ref, node_ref, w_in_ref, part_ref, cot_t_ref, node_part, w_edge_t
):
    latent = edge_ref.shape[1]

    @pl.when(pl.program_id(0) == 0)
    def _():
        node_part[...] = dot(w_in_ref[2 * latent :, :], node_ref[...], 0, 1).astype(BF)
        w_edge_t[...] = w_in_ref[:latent, :].T

    recv_hot = onehot_rows(node_ref.shape[0], recv_ref[0])
    part_ref[0] = dot(w_edge_t[...], edge_ref[...], 1, 1) + dot(node_part[...], recv_hot, 1, 0)
    cot_t_ref[0] = cot_ref[...].T


def prepare(edge_lat, edge_cot, recv_rows, node_lat, w_edge_in):
    edges, latent = edge_lat.shape
    hidden = w_edge_in.shape[1]
    nodes = node_lat.shape[0]
    chunks = edges // CHUNK
    rows = pl.BlockSpec((CHUNK, latent), lambda i: (i, 0))

    def along(height):
        return pl.BlockSpec((1, height, CHUNK), lambda i: (i, 0, 0))

    return pl.pallas_call(
        prepare_kernel,
        grid=(chunks,),
        out_shape=[
            pltpu.HBM((chunks, hidden, CHUNK), F32),
            pltpu.HBM((chunks, latent, CHUNK), BF),
        ],
        in_specs=[rows, rows, along(1), whole(node_lat.shape), whole(w_edge_in.shape)],
        out_specs=[along(hidden), along(latent)],
        scratch_shapes=[pltpu.VMEM((hidden, nodes), BF), pltpu.VMEM((hidden, latent), BF)],
        compiler_params=pltpu.CompilerParams(vmem_limit_bytes=VMEM_LIMIT),
        cost_estimate=pl.CostEstimate(
            flops=4 * edges * latent * hidden, bytes_accessed=8 * edges * latent, transcendentals=0
        ),
        name="prepare_edges",
    )(in_hbm(edge_lat), in_hbm(edge_cot), in_hbm(recv_rows), in_hbm(node_lat), in_hbm(w_edge_in))


def layer_kernel(
    piece_rows,
    core_ref,
    part_hbm,
    cot_hbm,
    edge_hbm,
    recv_ref,
    slot_ref,
    fetched_ref,
    wanted_ref,
    valid_ref,
    node_ref,
    node_cot_ref,
    w_in_ref,
    w_out_ref,
    gain_edge_ref,
    w_node_in_ref,
    w_node_out_ref,
    gain_node_ref,
    grad_pre_hbm,
    node_local_ref,
    keep_ref,
    send_ref,
    part,
    cot,
    edge,
    hot,
    hidden,
    slope,
    normed,
    scale,
    grad_pre,
    send_part,
    summed_acc,
    w_in_acc,
    w_out_acc,
    ends_acc,
    gain_acc,
    grad_summed,
    weight_pack,
    w_out_t,
    gain_column,
    sems,
    out_sems,
):
    chunks, latent, width = part.shape
    nodes = node_ref.shape[0]
    slots = fetched_ref.shape[0]
    stored = slots <= STORED_SLOTS
    bands = keep_ref.shape[0] * 2
    cap = slots // bands

    def part_copy(c):
        return pltpu.make_async_copy(part_hbm.at[c], part.at[c], sems.at[0, c])

    def cot_copy(c):
        return pltpu.make_async_copy(cot_hbm.at[c], cot.at[c], sems.at[1, c])

    def edge_copy(c):
        return pltpu.make_async_copy(edge_hbm.at[c], edge.at[c], sems.at[2, c])

    for copy in (part_copy, cot_copy, edge_copy):
        for c in range(chunks):
            copy(c).start()

    w_out_t[...] = w_out_ref[...].T
    gain_column[...] = jnp.broadcast_to(gain_edge_ref[...], (128, latent)).T
    summed_acc[...] = jnp.zeros_like(summed_acc)
    send_part[...] = dot(w_in_ref[latent : 2 * latent, :], fetched_ref[...], 0, 1).astype(BF)
    w_in_acc[...] = jnp.zeros_like(w_in_acc)
    w_out_acc[...] = jnp.zeros_like(w_out_acc)
    ends_acc[...] = jnp.zeros_like(ends_acc)
    gain_acc[...] = jnp.zeros_like(gain_acc)

    for c in range(chunks):
        for arrived in range(1) if c == 0 else range(1, chunks) if c == 1 else ():
            part_copy(arrived).wait()
        slot_hot = onehot_rows(slots, slot_ref[c])
        recv_hot = onehot_rows(nodes, recv_ref[c])
        hot[c, :nodes, :] = recv_hot
        if stored:
            hot[c, nodes:, :] = slot_hot
        pre = part[c] + dot(send_part[...], slot_hot, 1, 0)
        hid, slo = swish_and_slope(pre)
        hid = hid.astype(BF)
        hidden[c] = hid
        slope[c] = slo.astype(BF)
        out = dot(w_out_t[...], hid, 1, 0)
        centred = out - jnp.mean(out, axis=0, keepdims=True)
        inv = lax.rsqrt(jnp.mean(centred * centred, axis=0, keepdims=True) + epsilon)
        inv = inv * valid_ref[c]
        scale[c] = inv
        norm = (centred * inv).astype(BF)
        normed[c] = norm
        summed_acc[...] += dot(norm, recv_hot, 1, 1)

    for c in range(chunks):
        cot_copy(c).wait()
        edge_copy(c).wait()
    node = node_ref[...]
    summed = (summed_acc[...] * gain_column[:, :1]).astype(BF)
    pre_node = dot(w_node_in_ref[:latent, :], node, 0, 1) + dot(
        w_node_in_ref[latent:, :], summed, 0, 0
    )
    hid_node, slope_node = swish_and_slope(pre_node)
    hid_node = hid_node.astype(BF)
    out_node = dot(w_node_out_ref[...], hid_node, 0, 0)
    centred = out_node - jnp.mean(out_node, axis=0, keepdims=True)
    inv_node = lax.rsqrt(jnp.mean(centred * centred, axis=0, keepdims=True) + epsilon)
    norm_node = centred * inv_node
    node_base = node_cot_ref[...].astype(F32)
    cot_node = node_base.T
    product = cot_node * norm_node
    gain_node_grad = jnp.sum(product.T, axis=0, keepdims=True)
    dy = cot_node * jnp.broadcast_to(gain_node_ref[...], (128, latent)).T[:, :1]
    grad_out_node = (
        inv_node
        * (
            dy
            - jnp.mean(dy, axis=0, keepdims=True)
            - norm_node * jnp.mean(dy * norm_node, axis=0, keepdims=True)
        )
    ).astype(BF)
    base = 4 * latent
    weight_pack[base + 2 * latent : base + 3 * latent, :] = dot(hid_node, grad_out_node, 1, 1)
    grad_pre_node = (dot(w_node_out_ref[...], grad_out_node, 1, 0) * slope_node).astype(BF)
    weight_pack[base : base + latent, :] = dot(node, grad_pre_node, 0, 1)
    weight_pack[base + latent : base + 2 * latent, :] = dot(summed, grad_pre_node, 1, 1)
    grad_summed[...] = dot(w_node_in_ref[latent:, :], grad_pre_node, 1, 0).astype(BF)
    node_local = node_base + dot(grad_pre_node, w_node_in_ref[:latent, :], 0, 1)

    @pl.loop(0, chunks, unroll=True)
    def _(c):
        grad_update = cot[c].astype(F32) + dot(grad_summed[...], hot[c, :nodes, :], 1, 0)
        norm = normed[c].astype(F32)
        product = grad_update * norm
        gain_acc[...] += product
        gain = gain_column[:, :1]
        dy = grad_update * gain
        mean_dy = jnp.mean(dy, axis=0, keepdims=True)
        mean_product = jnp.mean(product * gain, axis=0, keepdims=True)
        grad_out = (scale[c] * (dy - mean_dy - norm * mean_product)).astype(BF)
        w_out_acc[...] += dot(hidden[c], grad_out, 1, 1)
        grad_hidden = dot(w_out_ref[...], grad_out, 1, 0)
        grad_in = (grad_hidden * slope[c].astype(F32)).astype(BF)
        grad_pre[c] = grad_in
        w_in_acc[...] += dot(grad_in, edge[c], 1, 0)
        if stored:
            ends_acc[...] += dot(hot[c], grad_in, 1, 1)
        else:
            ends_acc[:nodes, :] += dot(hot[c], grad_in, 1, 1)
            ends_acc[nodes:, :] += dot(onehot_rows(slots, slot_ref[c]), grad_in, 1, 1)

    for c in range(chunks):
        pltpu.make_async_copy(grad_pre.at[c], grad_pre_hbm.at[c], out_sems.at[c]).start()
    recv_sum = ends_acc[:nodes, :].astype(BF)
    slot_sum = ends_acc[nodes:, :].astype(BF)
    node_local_ref[...] = node_local + dot(recv_sum, w_in_ref[2 * latent :, :], 1, 1)
    weight_pack[:latent, :] = w_in_acc[...].T
    weight_pack[latent : 2 * latent, :] = dot(fetched_ref[...], slot_sum, 0, 0)
    weight_pack[2 * latent : 3 * latent, :] = dot(node, recv_sum, 0, 0)
    weight_pack[3 * latent : 4 * latent, :] = w_out_acc[...]
    used = base + 3 * latent
    if used < weight_pack.shape[0]:
        weight_pack[used:, :] = jnp.zeros_like(weight_pack[used:, :])
    gain_edge_grad = jnp.sum(gain_acc[...].T, axis=0, keepdims=True)
    slot_grads = dot(slot_sum, w_in_ref[latent : 2 * latent, :], 1, 1).astype(BF)
    core = core_ref[0]
    row = lax.broadcasted_iota(jnp.int32, (TAIL, latent), 0)
    column = lax.broadcasted_iota(jnp.int32, (1, latent), 1)
    for own in range(2):

        @pl.when(core == own)
        def _():
            for d in range(bands):
                out = (keep_ref if d % 2 == own else send_ref).at[d // 2]
                out[:cap, :] = slot_grads[d * cap : (d + 1) * cap, :]
                body = weight_pack[d * piece_rows : (d + 1) * piece_rows, :]
                out[cap : cap + piece_rows, :] = body.astype(BF)
                listed = jnp.concatenate(
                    [wanted_ref[d : d + 1, :].astype(F32)] * (latent // cap), axis=1
                )
                extra = jnp.where(row == 1, jnp.where(column // cap == own, listed, 0.0), 0.0)
                if d < 2:
                    extra = jnp.where(row == 0, gain_edge_grad if d == 0 else gain_node_grad, extra)
                out[cap + piece_rows :, :] = extra.astype(BF)

    for c in range(chunks):
        pltpu.make_async_copy(grad_pre.at[c], grad_pre_hbm.at[c], out_sems.at[c]).wait()


def layer(
    core, part, cot_t, edge_lat, recv_rows, slot_rows, fetched, wanted, valid_rows, node_lat, node_cot, weights, bands
):
    chunks, hidden, width = part.shape
    edges = edge_lat.reshape(chunks, width, -1)
    nodes, latent = node_lat.shape
    slots = fetched.shape[0]
    cap = slots // bands
    piece_rows = -(-7 * latent // (bands * 16)) * 16
    hbm = pl.BlockSpec(memory_space=pl.ANY)
    return pl.pallas_call(
        functools.partial(layer_kernel, piece_rows),
        out_shape=[
            pltpu.HBM((chunks, hidden, width), BF),
            jax.ShapeDtypeStruct((nodes, latent), F32),
            pltpu.VMEM((bands // 2, cap + piece_rows + TAIL, latent), BF),
            pltpu.VMEM((bands // 2, cap + piece_rows + TAIL, latent), BF),
        ],
        in_specs=[pl.BlockSpec(memory_space=pltpu.SMEM)] + [hbm] * 3 + [vmem()] * 13,
        out_specs=[hbm, vmem(), vmem(), vmem()],
        scratch_shapes=[
            pltpu.VMEM((chunks, hidden, width), F32),
            pltpu.VMEM((chunks, latent, width), BF),
            pltpu.VMEM((chunks, width, latent), BF),
            pltpu.VMEM((chunks, nodes + (slots if slots <= STORED_SLOTS else 0), width), BF),
            pltpu.VMEM((chunks, hidden, width), BF),
            pltpu.VMEM((chunks, hidden, width), BF),
            pltpu.VMEM((chunks, latent, width), BF),
            pltpu.VMEM((chunks, 1, width), F32),
            pltpu.VMEM((chunks, hidden, width), BF),
            pltpu.VMEM((hidden, slots), BF),
            pltpu.VMEM((latent, nodes), F32),
            pltpu.VMEM((hidden, latent), F32),
            pltpu.VMEM((hidden, latent), F32),
            pltpu.VMEM((nodes + slots, hidden), F32),
            pltpu.VMEM((latent, width), F32),
            pltpu.VMEM((latent, nodes), BF),
            pltpu.VMEM((piece_rows * bands, latent), F32),
            pltpu.VMEM((latent, hidden), BF),
            pltpu.VMEM((latent, 128), F32),
            pltpu.SemaphoreType.DMA((3, chunks)),
            pltpu.SemaphoreType.DMA((chunks,)),
        ],
        compiler_params=pltpu.CompilerParams(vmem_limit_bytes=LAYER_VMEM_LIMIT),
        name="layer_backward",
    )(core, in_hbm(part), in_hbm(cot_t), in_hbm(edges), recv_rows, slot_rows, in_vmem(fetched), wanted, valid_rows, node_lat, node_cot, *weights)


def edge_kernel(grad_ref, cot_ref, w_in_ref, out_ref):
    latent = cot_ref.shape[1]
    back = dot(grad_ref[0], w_in_ref[:latent, :], 0, 1)
    out_ref[...] = (cot_ref[...].astype(F32) + back).astype(BF)


def edge_result(grad_pre, edge_cot, w_edge_in):
    chunks, hidden, width = grad_pre.shape
    latent = edge_cot.shape[1]
    rows = pl.BlockSpec((width, latent), lambda i: (i, 0))
    return pl.pallas_call(
        edge_kernel,
        grid=(chunks,),
        out_shape=jax.ShapeDtypeStruct(edge_cot.shape, BF),
        in_specs=[
            pl.BlockSpec((1, hidden, width), lambda i: (i, 0, 0)),
            rows,
            whole(w_edge_in.shape),
        ],
        out_specs=rows,
        compiler_params=pltpu.CompilerParams(vmem_limit_bytes=VMEM_LIMIT),
        cost_estimate=pl.CostEstimate(
            flops=2 * chunks * width * hidden * latent,
            bytes_accessed=6 * chunks * width * latent,
            transcendentals=0,
        ),
        name="edge_result",
    )(in_hbm(grad_pre), in_hbm(edge_cot), w_edge_in)


def join_kernel(cap, keep_ref, got_ref, out_ref):
    out_ref[:, :cap, :] = keep_ref[:, :cap, :]
    out_ref[:, cap : 2 * cap, :] = got_ref[:, :cap, :]
    out_ref[:, 2 * cap :, :] = (
        keep_ref[:, cap:, :].astype(F32) + got_ref[:, cap:, :].astype(F32)
    ).astype(BF)


def join(keep, got, cap):
    chips, height, latent = keep.shape
    return pl.pallas_call(
        functools.partial(join_kernel, cap),
        out_shape=pltpu.VMEM((chips, height + cap, latent), BF),
        in_specs=[vmem(), vmem()],
        out_specs=vmem(),
        name="join_cores",
    )(in_vmem(keep), in_vmem(got))


def total_kernel(sums_ref, pieces_ref):
    chips, height, _ = pieces_ref.shape
    first = sums_ref.shape[1] - height
    piece = jnp.sum(sums_ref[:, first:, :].astype(F32), axis=0).astype(BF)
    for chip in range(chips):
        pieces_ref[chip] = piece


def total(sums, cap):
    chips, height, latent = sums.shape
    return pl.pallas_call(
        total_kernel,
        out_shape=pltpu.VMEM((chips, height - 2 * cap, latent), BF),
        in_specs=[vmem()],
        out_specs=vmem(),
        name="total_piece",
    )(in_vmem(sums))


def settle_kernel(cap, core_ref, back_ref, local_ref, node_grad_ref):
    chips, height, latent = back_ref.shape
    rows = back_ref[:, : 2 * cap, :].reshape(chips * 2 * cap, latent)
    core = core_ref[0]
    listed = back_ref[:, height - TAIL + 1, :].astype(F32)
    lists = []
    for chip in range(chips):
        first, second = listed[chip : chip + 1, :cap], listed[chip : chip + 1, cap : 2 * cap]
        lists.append(jnp.where(core == 0, first, second))
        lists.append(jnp.where(core == 0, second, first))
    picks = onehot_rows(local_ref.shape[0], jnp.concatenate(lists, axis=1).astype(jnp.int32))
    node_grad_ref[...] = local_ref[...] + dot(picks, rows, 1, 0)


def settle(place, back, node_local, cap):
    return pl.pallas_call(
        functools.partial(settle_kernel, cap),
        out_shape=jax.ShapeDtypeStruct(node_local.shape, F32),
        in_specs=[pl.BlockSpec(memory_space=pltpu.SMEM)] + [vmem()] * 2,
        out_specs=vmem(),
        name="settle_sums",
    )(place, in_vmem(back), node_local)


def assemble_kernel(core_ref, mine_ref, theirs_ref, *refs):
    outs, (rows, out_sems) = refs[:-2], refs[-2:]
    chips, height, latent = mine_ref.shape
    body = height - TAIL
    core = core_ref[0]
    starts, at = [], 0
    for out in outs[:-2]:
        starts.append(at)
        at += out.shape[0]

    def outgoing(k):
        source = rows.at[pl.ds(starts[k], outs[k].shape[0])]
        return pltpu.make_async_copy(source, outs[k], out_sems.at[k])

    sent = 0
    for chip in range(chips):
        for side, ref in enumerate((mine_ref, theirs_ref)):
            place = 2 * chip + (core if side == 0 else 1 - core)
            rows[pl.ds(pl.multiple_of(place * body, body), body), :] = ref[
                chip, :body, :
            ].astype(F32)
        if chip == 0:
            first, second = mine_ref[0, body:, :].astype(F32), theirs_ref[0, body:, :].astype(F32)
            outs[-2][...] = jnp.where(core == 0, first, second)[:1]
            outs[-1][...] = jnp.where(core == 0, second, first)[:1]
        while sent < len(starts) and starts[sent] + outs[sent].shape[0] <= 2 * (chip + 1) * body:
            outgoing(sent).start()
            sent += 1
    for k in range(len(starts)):
        outgoing(k).wait()


def assemble(place, mine, theirs, latent):
    chips, height, width = mine.shape
    heights = (3 * latent, latent, 2 * latent, latent, 1, 1)
    hbm = pl.BlockSpec(memory_space=pl.ANY)
    return pl.pallas_call(
        assemble_kernel,
        out_shape=[jax.ShapeDtypeStruct((rows, width), F32) for rows in heights],
        in_specs=[pl.BlockSpec(memory_space=pltpu.SMEM), vmem(), vmem()],
        out_specs=[hbm] * 4 + [vmem()] * 2,
        scratch_shapes=[
            pltpu.VMEM((2 * chips * (height - TAIL), width), F32),
            pltpu.SemaphoreType.DMA((4,)),
        ],
        compiler_params=pltpu.CompilerParams(vmem_limit_bytes=VMEM_LIMIT),
        name="assemble_sums",
    )(place, in_vmem(mine), in_vmem(theirs))


def per_device(
    node_lat,
    edge_lat,
    node_cot,
    edge_cot,
    w_edge_in,
    w_edge_out,
    gain_edge,
    w_node_in,
    w_node_out,
    gain_node,
    fetch_idx,
    edge_slot,
    edge_recv,
    block_fill,
):
    bands = lax.axis_size("band")
    chips = bands // 2
    me = lax.axis_index("band")
    place = jnp.stack([me % 2, me // GROUP, me]).astype(jnp.int32)
    latent = node_lat.shape[1]
    cap = fetch_idx.shape[2]
    slots = bands * cap
    chunks = edge_lat.shape[0] // CHUNK
    other_core = [(i, i ^ 1) for i in range(bands)]
    same_core = [[2 * i + c for i in range(chips)] for c in range(2)]

    groups = bands // GROUP
    like_placed = [[GROUP * g + i for g in range(groups)] for i in range(GROUP)]

    def swap(array, step):
        return lax.ppermute(array, "band", [(i, i ^ step) for i in range(bands)])

    lists = [fetch_idx]
    step = GROUP
    while step < bands:
        held = lists[0] if len(lists) == 1 else jnp.concatenate(lists, axis=0)
        lists.append(swap(held, step))
        step *= 2
    across = swap(node_lat, 2)
    members = (node_lat, swap(node_lat, 1), across, swap(across, 1))
    rows = serve(place, lists, members)
    valid = jnp.arange(128, dtype=jnp.int32)[None, :] < block_fill[0][:, None]
    valid = valid.astype(F32).reshape(chunks, 1, CHUNK)
    recv_rows = edge_recv.reshape(chunks, 1, CHUNK)
    w_edge_first, rows = lax.optimization_barrier((w_edge_in, rows))
    fetched = lax.all_to_all(
        rows, "band", split_axis=0, concat_axis=0, tiled=True, axis_index_groups=like_placed
    ).reshape(slots, latent)

    slot_rows = edge_slot.reshape(chunks, 1, CHUNK)
    part, cot_t = prepare(
        edge_lat, edge_cot, recv_rows, node_lat, w_edge_first
    )
    weights = (
        w_edge_in,
        w_edge_out,
        gain_edge[None, :],
        w_node_in,
        w_node_out,
        gain_node[None, :],
    )
    grad_pre, node_local, keep, send = layer(
        place,
        part,
        cot_t,
        edge_lat,
        recv_rows,
        slot_rows,
        fetched,
        fetch_idx[0],
        valid,
        node_lat,
        node_cot,
        weights,
        bands,
    )
    got = lax.ppermute(send, "band", other_core)
    joined = join(keep, got, cap)
    back = lax.all_to_all(
        joined, "band", split_axis=0, concat_axis=0, tiled=True, axis_index_groups=same_core
    )
    edge_grad = edge_result(grad_pre, edge_cot, w_edge_in)
    back, edge_grad = lax.optimization_barrier((back, edge_grad))
    pieces = total(back, cap)
    mine = lax.all_to_all(
        pieces, "band", split_axis=0, concat_axis=0, tiled=True, axis_index_groups=same_core
    )
    node_grad = settle(place, back, node_local, cap)
    mine, node_grad = lax.optimization_barrier((mine, node_grad))
    theirs = lax.ppermute(mine, "band", other_core)
    sums = assemble(place, mine, theirs, latent)
    return (
        node_grad,
        edge_grad,
        sums[0],
        sums[1],
        sums[4].reshape(-1),
        sums[2],
        sums[3],
        sums[5].reshape(-1),
    )


def solution(mesh):
    in_specs = (
        P(("grp", "band"), None),
        P(("grp", "band"), None),
        P(("grp", "band"), None),
        P(("grp", "band"), None),
        P(),
        P(),
        P(),
        P(),
        P(),
        P(),
        P("band", None, None),
        P("band"),
        P("band"),
        P("band", None),
    )
    out_specs = (
        P(("grp", "band"), None),
        P(("grp", "band"), None),
        P("grp", None),
        P("grp", None),
        P("grp"),
        P("grp", None),
        P("grp", None),
        P("grp"),
    )
    return jax.shard_map(
        per_device, mesh=mesh, in_specs=in_specs, out_specs=out_specs, check_vma=False
    )
```

```python
import functools

import jax
import jax.numpy as jnp
from jax import lax
from jax.experimental import pallas as pl
from jax.experimental.pallas import tpu as pltpu
from jax.sharding import PartitionSpec as P

epsilon = 1e-05
CHUNK = 1280
GROUP = 4
TAIL = 8
VMEM_LIMIT = 20 * 2**20
LAYER_VMEM_LIMIT = 48 * 2**20
STORED_SLOTS = 1024
BF = jnp.bfloat16
F32 = jnp.float32


def dot(lhs, rhs, lhs_dim, rhs_dim):
    return lax.dot_general(
        lhs, rhs, (((lhs_dim,), (rhs_dim,)), ((), ())), preferred_element_type=F32
    )


def swish_and_slope(values):
    logistic = jax.nn.sigmoid(values)
    hidden = values * logistic
    return hidden, logistic + hidden * (1.0 - logistic)


def onehot_rows(row_count, index_row):
    rows = lax.broadcasted_iota(jnp.int16, (row_count, index_row.shape[1]), 0)
    return jnp.where(rows == index_row.astype(jnp.int16), jnp.ones((), BF), jnp.zeros((), BF))


def in_vmem(array):
    return pltpu.with_memory_space_constraint(array, pltpu.VMEM)


def in_hbm(array):
    return pltpu.with_memory_space_constraint(array, pltpu.HBM)


def vmem():
    return pl.BlockSpec(memory_space=pltpu.VMEM)


def whole(shape):
    return pl.BlockSpec(shape, lambda *_: (0,) * len(shape))


def serve_kernel(place_ref, *refs):
    members, lists, rows_ref = refs[:GROUP], refs[GROUP:-1], refs[-1]
    entries = [ref.at[i] for ref in lists for i in range(ref.shape[0])]
    groups, cap = len(entries), entries[0].shape[1]
    group, member = place_ref[1], place_ref[2] % GROUP
    for k, nodes_ref in enumerate(members):
        owner = member ^ k
        wanted = jnp.concatenate(
            [entry[pl.ds(group * GROUP + owner, 1), :] for entry in entries], axis=1
        )
        picks = onehot_rows(nodes_ref.shape[0], wanted)
        rows = dot(picks, nodes_ref[...], 0, 0).astype(BF)
        place = pl.ds(pl.multiple_of(owner * cap, cap), cap)
        for j in range(groups):
            rows_ref[group ^ j, place, :] = rows[j * cap : (j + 1) * cap]


def serve(place, lists, members):
    groups, cap = sum(part.shape[0] for part in lists), lists[0].shape[2]
    return pl.pallas_call(
        serve_kernel,
        out_shape=pltpu.VMEM((groups, GROUP * cap, members[0].shape[1]), BF),
        in_specs=[pl.BlockSpec(memory_space=pltpu.SMEM)] + [vmem()] * (GROUP + len(lists)),
        out_specs=vmem(),
        compiler_params=pltpu.CompilerParams(vmem_limit_bytes=VMEM_LIMIT),
        name="serve_rows",
    )(place, in_hbm(members[0]), *map(in_vmem, members[1:]), in_hbm(lists[0]), *map(in_vmem, lists[1:]))


def prepare_kernel(
    edge_ref, cot_ref, recv_ref, node_ref, w_in_ref, part_ref, cot_t_ref, node_part, w_edge_t
):
    latent = edge_ref.shape[1]

    @pl.when(pl.program_id(0) == 0)
    def _():
        node_part[...] = dot(w_in_ref[2 * latent :, :], node_ref[...], 0, 1).astype(BF)
        w_edge_t[...] = w_in_ref[:latent, :].T

    recv_hot = onehot_rows(node_ref.shape[0], recv_ref[0])
    part_ref[0] = dot(w_edge_t[...], edge_ref[...], 1, 1) + dot(node_part[...], recv_hot, 1, 0)
    cot_t_ref[0] = cot_ref[...].T


def prepare(edge_lat, edge_cot, recv_rows, node_lat, w_edge_in):
    edges, latent = edge_lat.shape
    hidden = w_edge_in.shape[1]
    nodes = node_lat.shape[0]
    chunks = edges // CHUNK
    rows = pl.BlockSpec((CHUNK, latent), lambda i: (i, 0))

    def along(height):
        return pl.BlockSpec((1, height, CHUNK), lambda i: (i, 0, 0))

    return pl.pallas_call(
        prepare_kernel,
        grid=(chunks,),
        out_shape=[
            pltpu.HBM((chunks, hidden, CHUNK), F32),
            pltpu.HBM((chunks, latent, CHUNK), BF),
        ],
        in_specs=[rows, rows, along(1), whole(node_lat.shape), whole(w_edge_in.shape)],
        out_specs=[along(hidden), along(latent)],
        scratch_shapes=[pltpu.VMEM((hidden, nodes), BF), pltpu.VMEM((hidden, latent), BF)],
        compiler_params=pltpu.CompilerParams(vmem_limit_bytes=VMEM_LIMIT),
        cost_estimate=pl.CostEstimate(
            flops=4 * edges * latent * hidden, bytes_accessed=8 * edges * latent, transcendentals=0
        ),
        name="prepare_edges",
    )(in_hbm(edge_lat), in_hbm(edge_cot), in_hbm(recv_rows), in_hbm(node_lat), in_hbm(w_edge_in))


def layer_kernel(
    piece_rows,
    core_ref,
    part_hbm,
    cot_hbm,
    edge_hbm,
    recv_ref,
    slot_ref,
    fetched_ref,
    wanted_ref,
    valid_ref,
    node_ref,
    node_cot_ref,
    w_in_ref,
    w_out_ref,
    gain_edge_ref,
    w_node_in_ref,
    w_node_out_ref,
    gain_node_ref,
    grad_pre_hbm,
    node_local_ref,
    keep_ref,
    send_ref,
    part,
    cot,
    edge,
    hot,
    hidden,
    slope,
    normed,
    scale,
    grad_pre,
    send_part,
    summed_acc,
    w_in_acc,
    w_out_acc,
    ends_acc,
    gain_acc,
    grad_summed,
    weight_pack,
    w_out_t,
    gain_column,
    sems,
    out_sems,
):
    chunks, latent, width = part.shape
    nodes = node_ref.shape[0]
    slots = fetched_ref.shape[0]
    stored = slots <= STORED_SLOTS
    bands = keep_ref.shape[0] * 2
    cap = slots // bands

    def part_copy(c):
        return pltpu.make_async_copy(part_hbm.at[c], part.at[c], sems.at[0, c])

    def cot_copy(c):
        return pltpu.make_async_copy(cot_hbm.at[c], cot.at[c], sems.at[1, c])

    def edge_copy(c):
        return pltpu.make_async_copy(edge_hbm.at[c], edge.at[c], sems.at[2, c])

    for copy in (part_copy, cot_copy, edge_copy):
        for c in range(chunks):
            copy(c).start()

    w_out_t[...] = w_out_ref[...].T
    gain_column[...] = jnp.broadcast_to(gain_edge_ref[...], (128, latent)).T
    summed_acc[...] = jnp.zeros_like(summed_acc)
    send_part[...] = dot(w_in_ref[latent : 2 * latent, :], fetched_ref[...], 0, 1).astype(BF)
    w_in_acc[...] = jnp.zeros_like(w_in_acc)
    w_out_acc[...] = jnp.zeros_like(w_out_acc)
    ends_acc[...] = jnp.zeros_like(ends_acc)
    gain_acc[...] = jnp.zeros_like(gain_acc)

    for c in range(chunks):
        for arrived in range(1) if c == 0 else range(1, chunks) if c == 1 else ():
            part_copy(arrived).wait()
        slot_hot = onehot_rows(slots, slot_ref[c])
        recv_hot = onehot_rows(nodes, recv_ref[c])
        hot[c, :nodes, :] = recv_hot
        if stored:
            hot[c, nodes:, :] = slot_hot
        pre = part[c] + dot(send_part[...], slot_hot, 1, 0)
        hid, slo = swish_and_slope(pre)
        hid = hid.astype(BF)
        hidden[c] = hid
        slope[c] = slo.astype(BF)
        out = dot(w_out_t[...], hid, 1, 0)
        centred = out - jnp.mean(out, axis=0, keepdims=True)
        inv = lax.rsqrt(jnp.mean(centred * centred, axis=0, keepdims=True) + epsilon)
        inv = inv * valid_ref[c]
        scale[c] = inv
        norm = (centred * inv).astype(BF)
        normed[c] = norm
        summed_acc[...] += dot(norm, recv_hot, 1, 1)

    for c in range(chunks):
        cot_copy(c).wait()
        edge_copy(c).wait()
    node = node_ref[...]
    summed = (summed_acc[...] * gain_column[:, :1]).astype(BF)
    pre_node = dot(w_node_in_ref[:latent, :], node, 0, 1) + dot(
        w_node_in_ref[latent:, :], summed, 0, 0
    )
    hid_node, slope_node = swish_and_slope(pre_node)
    hid_node = hid_node.astype(BF)
    out_node = dot(w_node_out_ref[...], hid_node, 0, 0)
    centred = out_node - jnp.mean(out_node, axis=0, keepdims=True)
    inv_node = lax.rsqrt(jnp.mean(centred * centred, axis=0, keepdims=True) + epsilon)
    norm_node = centred * inv_node
    node_base = node_cot_ref[...].astype(F32)
    cot_node = node_base.T
    product = cot_node * norm_node
    gain_node_grad = jnp.sum(product.T, axis=0, keepdims=True)
    dy = cot_node * jnp.broadcast_to(gain_node_ref[...], (128, latent)).T[:, :1]
    grad_out_node = (
        inv_node
        * (
            dy
            - jnp.mean(dy, axis=0, keepdims=True)
            - norm_node * jnp.mean(dy * norm_node, axis=0, keepdims=True)
        )
    ).astype(BF)
    base = 4 * latent
    weight_pack[base + 2 * latent : base + 3 * latent, :] = dot(hid_node, grad_out_node, 1, 1)
    grad_pre_node = (dot(w_node_out_ref[...], grad_out_node, 1, 0) * slope_node).astype(BF)
    weight_pack[base : base + latent, :] = dot(node, grad_pre_node, 0, 1)
    weight_pack[base + latent : base + 2 * latent, :] = dot(summed, grad_pre_node, 1, 1)
    grad_summed[...] = dot(w_node_in_ref[latent:, :], grad_pre_node, 1, 0).astype(BF)
    node_local = node_base + dot(grad_pre_node, w_node_in_ref[:latent, :], 0, 1)

    @pl.loop(0, chunks, unroll=True)
    def _(c):
        grad_update = cot[c].astype(F32) + dot(grad_summed[...], hot[c, :nodes, :], 1, 0)
        norm = normed[c].astype(F32)
        product = grad_update * norm
        gain_acc[...] += product
        gain = gain_column[:, :1]
        dy = grad_update * gain
        mean_dy = jnp.mean(dy, axis=0, keepdims=True)
        mean_product = jnp.mean(product * gain, axis=0, keepdims=True)
        grad_out = (scale[c] * (dy - mean_dy - norm * mean_product)).astype(BF)
        w_out_acc[...] += dot(hidden[c], grad_out, 1, 1)
        grad_hidden = dot(w_out_ref[...], grad_out, 1, 0)
        grad_in = (grad_hidden * slope[c].astype(F32)).astype(BF)
        grad_pre[c] = grad_in
        w_in_acc[...] += dot(grad_in, edge[c], 1, 0)
        if stored:
            ends_acc[...] += dot(hot[c], grad_in, 1, 1)
        else:
            ends_acc[:nodes, :] += dot(hot[c], grad_in, 1, 1)
            ends_acc[nodes:, :] += dot(onehot_rows(slots, slot_ref[c]), grad_in, 1, 1)

    for c in range(chunks):
        pltpu.make_async_copy(grad_pre.at[c], grad_pre_hbm.at[c], out_sems.at[c]).start()
    recv_sum = ends_acc[:nodes, :].astype(BF)
    slot_sum = ends_acc[nodes:, :].astype(BF)
    node_local_ref[...] = node_local + dot(recv_sum, w_in_ref[2 * latent :, :], 1, 1)
    weight_pack[:latent, :] = w_in_acc[...].T
    weight_pack[latent : 2 * latent, :] = dot(fetched_ref[...], slot_sum, 0, 0)
    weight_pack[2 * latent : 3 * latent, :] = dot(node, recv_sum, 0, 0)
    weight_pack[3 * latent : 4 * latent, :] = w_out_acc[...]
    used = base + 3 * latent
    if used < weight_pack.shape[0]:
        weight_pack[used:, :] = jnp.zeros_like(weight_pack[used:, :])
    gain_edge_grad = jnp.sum(gain_acc[...].T, axis=0, keepdims=True)
    slot_grads = dot(slot_sum, w_in_ref[latent : 2 * latent, :], 1, 1).astype(BF)
    core = core_ref[0]
    row = lax.broadcasted_iota(jnp.int32, (TAIL, latent), 0)
    column = lax.broadcasted_iota(jnp.int32, (1, latent), 1)
    for own in range(2):

        @pl.when(core == own)
        def _():
            for d in range(bands):
                out = (keep_ref if d % 2 == own else send_ref).at[d // 2]
                out[:cap, :] = slot_grads[d * cap : (d + 1) * cap, :]
                body = weight_pack[d * piece_rows : (d + 1) * piece_rows, :]
                out[cap : cap + piece_rows, :] = body.astype(BF)
                listed = jnp.concatenate(
                    [wanted_ref[d : d + 1, :].astype(F32)] * (latent // cap), axis=1
                )
                extra = jnp.where(row == 1, jnp.where(column // cap == own, listed, 0.0), 0.0)
                if d < 2:
                    extra = jnp.where(row == 0, gain_edge_grad if d == 0 else gain_node_grad, extra)
                out[cap + piece_rows :, :] = extra.astype(BF)

    for c in range(chunks):
        pltpu.make_async_copy(grad_pre.at[c], grad_pre_hbm.at[c], out_sems.at[c]).wait()


def layer(
    core, part, cot_t, edge_lat, recv_rows, slot_rows, fetched, wanted, valid_rows, node_lat, node_cot, weights, bands
):
    chunks, hidden, width = part.shape
    edges = edge_lat.reshape(chunks, width, -1)
    nodes, latent = node_lat.shape
    slots = fetched.shape[0]
    cap = slots // bands
    piece_rows = -(-7 * latent // (bands * 16)) * 16
    hbm = pl.BlockSpec(memory_space=pl.ANY)
    return pl.pallas_call(
        functools.partial(layer_kernel, piece_rows),
        out_shape=[
            pltpu.HBM((chunks, hidden, width), BF),
            pltpu.VMEM((nodes, latent), F32),
            pltpu.VMEM((bands // 2, cap + piece_rows + TAIL, latent), BF),
            pltpu.VMEM((bands // 2, cap + piece_rows + TAIL, latent), BF),
        ],
        in_specs=[pl.BlockSpec(memory_space=pltpu.SMEM)] + [hbm] * 3 + [vmem()] * 13,
        out_specs=[hbm, vmem(), vmem(), vmem()],
        scratch_shapes=[
            pltpu.VMEM((chunks, hidden, width), F32),
            pltpu.VMEM((chunks, latent, width), BF),
            pltpu.VMEM((chunks, width, latent), BF),
            pltpu.VMEM((chunks, nodes + (slots if slots <= STORED_SLOTS else 0), width), BF),
            pltpu.VMEM((chunks, hidden, width), BF),
            pltpu.VMEM((chunks, hidden, width), BF),
            pltpu.VMEM((chunks, latent, width), BF),
            pltpu.VMEM((chunks, 1, width), F32),
            pltpu.VMEM((chunks, hidden, width), BF),
            pltpu.VMEM((hidden, slots), BF),
            pltpu.VMEM((latent, nodes), F32),
            pltpu.VMEM((hidden, latent), F32),
            pltpu.VMEM((hidden, latent), F32),
            pltpu.VMEM((nodes + slots, hidden), F32),
            pltpu.VMEM((latent, width), F32),
            pltpu.VMEM((latent, nodes), BF),
            pltpu.VMEM((piece_rows * bands, latent), F32),
            pltpu.VMEM((latent, hidden), BF),
            pltpu.VMEM((latent, 128), F32),
            pltpu.SemaphoreType.DMA((3, chunks)),
            pltpu.SemaphoreType.DMA((chunks,)),
        ],
        compiler_params=pltpu.CompilerParams(vmem_limit_bytes=LAYER_VMEM_LIMIT),
        name="layer_backward",
    )(core, in_hbm(part), in_hbm(cot_t), in_hbm(edges), recv_rows, slot_rows, in_vmem(fetched), wanted, valid_rows, node_lat, node_cot, *weights)


def edge_kernel(grad_ref, cot_ref, w_in_ref, out_ref):
    latent = cot_ref.shape[1]
    back = dot(grad_ref[0], w_in_ref[:latent, :], 0, 1)
    out_ref[...] = (cot_ref[...].astype(F32) + back).astype(BF)


def edge_result(grad_pre, edge_cot, w_edge_in):
    chunks, hidden, width = grad_pre.shape
    latent = edge_cot.shape[1]
    rows = pl.BlockSpec((width, latent), lambda i: (i, 0))
    return pl.pallas_call(
        edge_kernel,
        grid=(chunks,),
        out_shape=jax.ShapeDtypeStruct(edge_cot.shape, BF),
        in_specs=[
            pl.BlockSpec((1, hidden, width), lambda i: (i, 0, 0)),
            rows,
            whole(w_edge_in.shape),
        ],
        out_specs=rows,
        compiler_params=pltpu.CompilerParams(vmem_limit_bytes=VMEM_LIMIT),
        cost_estimate=pl.CostEstimate(
            flops=2 * chunks * width * hidden * latent,
            bytes_accessed=6 * chunks * width * latent,
            transcendentals=0,
        ),
        name="edge_result",
    )(in_hbm(grad_pre), in_hbm(edge_cot), w_edge_in)


def join_kernel(cap, keep_ref, got_ref, out_ref):
    out_ref[:, :cap, :] = keep_ref[:, :cap, :]
    out_ref[:, cap : 2 * cap, :] = got_ref[:, :cap, :]
    out_ref[:, 2 * cap :, :] = (
        keep_ref[:, cap:, :].astype(F32) + got_ref[:, cap:, :].astype(F32)
    ).astype(BF)


def join(keep, got, cap):
    chips, height, latent = keep.shape
    return pl.pallas_call(
        functools.partial(join_kernel, cap),
        out_shape=pltpu.VMEM((chips, height + cap, latent), BF),
        in_specs=[vmem(), vmem()],
        out_specs=vmem(),
        name="join_cores",
    )(in_vmem(keep), in_vmem(got))


def total_kernel(sums_ref, pieces_ref):
    chips, height, _ = pieces_ref.shape
    first = sums_ref.shape[1] - height
    piece = jnp.sum(sums_ref[:, first:, :].astype(F32), axis=0).astype(BF)
    for chip in range(chips):
        pieces_ref[chip] = piece


def total(sums, cap):
    chips, height, latent = sums.shape
    return pl.pallas_call(
        total_kernel,
        out_shape=pltpu.VMEM((chips, height - 2 * cap, latent), BF),
        in_specs=[vmem()],
        out_specs=vmem(),
        name="total_piece",
    )(in_vmem(sums))


def settle_kernel(cap, core_ref, back_ref, local_ref, node_grad_ref):
    chips, height, latent = back_ref.shape
    rows = back_ref[:, : 2 * cap, :].reshape(chips * 2 * cap, latent)
    core = core_ref[0]
    listed = back_ref[:, height - TAIL + 1, :].astype(F32)
    lists = []
    for chip in range(chips):
        first, second = listed[chip : chip + 1, :cap], listed[chip : chip + 1, cap : 2 * cap]
        lists.append(jnp.where(core == 0, first, second))
        lists.append(jnp.where(core == 0, second, first))
    picks = onehot_rows(local_ref.shape[0], jnp.concatenate(lists, axis=1).astype(jnp.int32))
    node_grad_ref[...] = local_ref[...] + dot(picks, rows, 1, 0)


def settle(place, back, node_local, cap):
    return pl.pallas_call(
        functools.partial(settle_kernel, cap),
        out_shape=jax.ShapeDtypeStruct(node_local.shape, F32),
        in_specs=[pl.BlockSpec(memory_space=pltpu.SMEM)] + [vmem()] * 2,
        out_specs=vmem(),
        name="settle_sums",
    )(place, in_vmem(back), in_vmem(node_local))


def assemble_kernel(core_ref, mine_ref, theirs_ref, *refs):
    outs, (rows, out_sems) = refs[:-2], refs[-2:]
    chips, height, latent = mine_ref.shape
    body = height - TAIL
    core = core_ref[0]
    starts, at = [], 0
    for out in outs[:-2]:
        starts.append(at)
        at += out.shape[0]

    def outgoing(k):
        source = rows.at[pl.ds(starts[k], outs[k].shape[0])]
        return pltpu.make_async_copy(source, outs[k], out_sems.at[k])

    sent = 0
    for chip in range(chips):
        for side, ref in enumerate((mine_ref, theirs_ref)):
            place = 2 * chip + (core if side == 0 else 1 - core)
            rows[pl.ds(pl.multiple_of(place * body, body), body), :] = ref[
                chip, :body, :
            ].astype(F32)
        if chip == 0:
            first, second = mine_ref[0, body:, :].astype(F32), theirs_ref[0, body:, :].astype(F32)
            outs[-2][...] = jnp.where(core == 0, first, second)[:1]
            outs[-1][...] = jnp.where(core == 0, second, first)[:1]
        while sent < len(starts) and starts[sent] + outs[sent].shape[0] <= 2 * (chip + 1) * body:
            outgoing(sent).start()
            sent += 1
    for k in range(len(starts)):
        outgoing(k).wait()


def assemble(place, mine, theirs, latent):
    chips, height, width = mine.shape
    heights = (3 * latent, latent, 2 * latent, latent, 1, 1)
    hbm = pl.BlockSpec(memory_space=pl.ANY)
    return pl.pallas_call(
        assemble_kernel,
        out_shape=[jax.ShapeDtypeStruct((rows, width), F32) for rows in heights],
        in_specs=[pl.BlockSpec(memory_space=pltpu.SMEM), vmem(), vmem()],
        out_specs=[hbm] * 4 + [vmem()] * 2,
        scratch_shapes=[
            pltpu.VMEM((2 * chips * (height - TAIL), width), F32),
            pltpu.SemaphoreType.DMA((4,)),
        ],
        compiler_params=pltpu.CompilerParams(vmem_limit_bytes=VMEM_LIMIT),
        name="assemble_sums",
    )(place, in_vmem(mine), in_vmem(theirs))


def per_device(
    node_lat,
    edge_lat,
    node_cot,
    edge_cot,
    w_edge_in,
    w_edge_out,
    gain_edge,
    w_node_in,
    w_node_out,
    gain_node,
    fetch_idx,
    edge_slot,
    edge_recv,
    block_fill,
):
    bands = lax.axis_size("band")
    chips = bands // 2
    me = lax.axis_index("band")
    place = jnp.stack([me % 2, me // GROUP, me]).astype(jnp.int32)
    latent = node_lat.shape[1]
    cap = fetch_idx.shape[2]
    slots = bands * cap
    chunks = edge_lat.shape[0] // CHUNK
    other_core = [(i, i ^ 1) for i in range(bands)]
    same_core = [[2 * i + c for i in range(chips)] for c in range(2)]

    groups = bands // GROUP
    like_placed = [[GROUP * g + i for g in range(groups)] for i in range(GROUP)]

    def swap(array, step):
        return lax.ppermute(array, "band", [(i, i ^ step) for i in range(bands)])

    lists = [fetch_idx]
    step = GROUP
    while step < bands:
        held = lists[0] if len(lists) == 1 else jnp.concatenate(lists, axis=0)
        lists.append(swap(held, step))
        step *= 2
    across = swap(node_lat, 2)
    members = (node_lat, swap(node_lat, 1), across, swap(across, 1))
    rows = serve(place, lists, members)
    valid = jnp.arange(128, dtype=jnp.int32)[None, :] < block_fill[0][:, None]
    valid = valid.astype(F32).reshape(chunks, 1, CHUNK)
    recv_rows = edge_recv.reshape(chunks, 1, CHUNK)
    w_edge_first, rows = lax.optimization_barrier((w_edge_in, rows))
    fetched = lax.all_to_all(
        rows, "band", split_axis=0, concat_axis=0, tiled=True, axis_index_groups=like_placed
    ).reshape(slots, latent)

    slot_rows = edge_slot.reshape(chunks, 1, CHUNK)
    part, cot_t = prepare(
        edge_lat, edge_cot, recv_rows, node_lat, w_edge_first
    )
    weights = (
        w_edge_in,
        w_edge_out,
        gain_edge[None, :],
        w_node_in,
        w_node_out,
        gain_node[None, :],
    )
    grad_pre, node_local, keep, send = layer(
        place,
        part,
        cot_t,
        edge_lat,
        recv_rows,
        slot_rows,
        fetched,
        fetch_idx[0],
        valid,
        node_lat,
        node_cot,
        weights,
        bands,
    )
    got = lax.ppermute(send, "band", other_core)
    joined = join(keep, got, cap)
    back = lax.all_to_all(
        joined, "band", split_axis=0, concat_axis=0, tiled=True, axis_index_groups=same_core
    )
    edge_grad = edge_result(grad_pre, edge_cot, w_edge_in)
    back, edge_grad = lax.optimization_barrier((back, edge_grad))
    pieces = total(back, cap)
    mine = lax.all_to_all(
        pieces, "band", split_axis=0, concat_axis=0, tiled=True, axis_index_groups=same_core
    )
    node_grad = settle(place, back, node_local, cap)
    mine, node_grad = lax.optimization_barrier((mine, node_grad))
    theirs = lax.ppermute(mine, "band", other_core)
    sums = assemble(place, mine, theirs, latent)
    return (
        node_grad,
        edge_grad,
        sums[0],
        sums[1],
        sums[4].reshape(-1),
        sums[2],
        sums[3],
        sums[5].reshape(-1),
    )


def solution(mesh):
    in_specs = (
        P(("grp", "band"), None),
        P(("grp", "band"), None),
        P(("grp", "band"), None),
        P(("grp", "band"), None),
        P(),
        P(),
        P(),
        P(),
        P(),
        P(),
        P("band", None, None),
        P("band"),
        P("band"),
        P("band", None),
    )
    out_specs = (
        P(("grp", "band"), None),
        P(("grp", "band"), None),
        P("grp", None),
        P("grp", None),
        P("grp"),
        P("grp", None),
        P("grp", None),
        P("grp"),
    )
    return jax.shard_map(
        per_device, mesh=mesh, in_specs=in_specs, out_specs=out_specs, check_vma=False
    )
```
